32 devices in a mesh: pair: 8 (over z, x), aux: 4 (over y, core).
Axes of the slice: x: 2, y: 2, z: 4, core: 2. Of those that a mesh axis runs over, the one named last changes fastest.
Arguments:
- amps: bfloat16 [256, 128, 128], P(('pair', 'aux')), may hold values from -6 to 6
- rotation: bfloat16 [256, 128, 128], P(('pair', 'aux')), may hold values from -0.5 to 0.5
- intersections: bfloat16 [256, 4, 128, 128], P(('pair', 'aux')), may hold values from -0.5 to 0.5
- energies: float32 [256, 128], P(('pair', 'aux')), may hold values from 0.25 to 2
- domains: int32 [256, 2], P(('pair', 'aux')), may hold values from 0 to 7
- owners: int32 [256, 4], P(('pair', 'aux')), may hold values from 0 to 7, all different within a row; in each aligned block of 8 rows (0 to 7, 8 to 15, ...) at most 8 rows name the same one
- slots: int32 [256, 4], P(('pair', 'aux')), may hold values from 0 to 7
- tiles: int32 [256], P(('pair', 'aux')), may hold values from 0 to 7
- blocks: bfloat16 [8, 512, 128], P('aux'), may hold values from -3 to 3
- coeffs: bfloat16 [8, 128, 4096], P('pair', None, 'aux'), may hold values from -0.5 to 0.5
Outputs:
- new_amps: bfloat16 [256, 128, 128], P(('pair', 'aux'))
- density: float32 [8, 128, 4096], P('pair', None, 'aux')
The draws below stay inside these ranges and needn't reach their ends.
Inputs may be any that keep to these rules, and one draw needn't show every extreme that they name: Each row names distinct owners; among the rows of one device no owner is named by more than 8 entries, a bound that some block reaches.
All inputs are finite; a program needn't handle non-finite values.
Results may differ from the reference program's by a relative error of at most 0.014.
Values may be sent and summed in bfloat16 or wider, within the bound.
A program may use at most 64 MiB of HBM per device.

```python
import math
import jax
import jax.numpy as jnp
import numpy as np
from jax import lax

VIRTUALS = 128
AUX_FUNCS = 512
AO_WIDTH = 4096
NEIGHBOURS = 4
PAIR_DEV = 8
PAIRS = 256
CAPACITY = 8
BLOCKS = 8
TILES = 8
N_PAIR = 8
N_AUX = 4


def with_ends(values, rng, smallest, top_value):
    longest = values.shape.index(max(values.shape))
    spots = []
    for shift in (0, 1):
        where = [jax.random.randint(jax.random.fold_in(rng, axis), (), 0, length) for axis, length in enumerate(values.shape)]
        where[longest] = (where[longest] + shift) % values.shape[longest]
        spots.append(tuple(where))
    return values.at[spots[0]].set(smallest).at[spots[1]].set(top_value)


def block_levels(rng, dims, pieces, smallest, largest):
    def one(dim, shards_of):
        heights = jax.random.uniform(jax.random.fold_in(jax.random.fold_in(rng, 6), dim), (shards_of,), jnp.float32, smallest / len(pieces), largest / len(pieces))
        return jnp.repeat(jnp.exp(heights), dims[dim] // shards_of).reshape((-1,) + (1,) * (len(dims) - dim - 1))

    factor_of = one(*pieces[0])
    for cut in pieces[1:]:
        factor_of = factor_of * one(*cut)
    return factor_of


def assign_block(rng, own, number, rows, number_of, top, limit, slope):
    sequence = jax.random.permutation(rng, number_of)
    packed, common = shares(number_of, rows * top, limit, slope, True), shares(number_of, rows * top, limit, slope, False)
    places = jnp.arange(number_of)

    def named(lengths, offset_by):
        used = int((lengths > 0).sum())
        fixed = max(1, used // 4)
        shifted = fixed + (places - fixed + offset_by * (used - fixed)) % max(1, number_of - fixed)
        return jnp.zeros((number_of,), jnp.int32).at[sequence[jnp.where(places < fixed, places, shifted)]].set(jnp.asarray(lengths, jnp.int32))

    lengths = jnp.where(number % 4 == 0, named(packed, number // 4), named(common, number - number // 4 - 1))
    mixed = jax.random.permutation(jax.random.fold_in(own, 3), number_of)
    giver, receiver = mixed[0:number_of // 2 * 2:2], mixed[1:number_of // 2 * 2:2]
    room = jnp.minimum(lengths[giver] - 1, limit - lengths[receiver]) // 2
    room = jnp.where((giver == sequence[0]) | (receiver == sequence[0]) | (lengths[receiver] == 0), 0, jnp.maximum(room, 0))
    shifted = jax.random.randint(jax.random.fold_in(own, 4), (number_of // 2,), 0, 1 << 20) % (room + 1)
    lengths = lengths.at[giver].add(-shifted).at[receiver].add(shifted)
    members = jnp.searchsorted(jnp.cumsum(lengths), jnp.arange(rows * top), side="right").astype(jnp.int32)
    listing = members.reshape(top, rows).T
    listing = listing[jax.random.permutation(jax.random.fold_in(own, 1), rows)]
    offset_by = jax.random.randint(jax.random.fold_in(own, 2), (rows, 1), 0, top)
    return jnp.take_along_axis(listing, (jnp.arange(top)[None, :] + offset_by) % top, axis=1)


def shares(number_of, total, most, skew, full):
    loads = [(1 << 20) // math.isqrt(rank ** skew) + 1 for rank in range(1, number_of + 1)]
    largest = most if full else min(most, max(-(-total // number_of), total * loads[0] // sum(loads)))
    least = 1 if total - largest >= number_of - 1 else 0
    counts, rest = [largest] + [least] * (number_of - 1), total - largest - least * (number_of - 1)
    while rest > 0:
        free = [i for i in range(1, number_of) if counts[i] < largest] or [i for i in range(1, number_of) if counts[i] < most]
        pool, remaining = sum([loads[i] for i in free]), rest
        for i in free:
            addition = min(most - counts[i], max(1, remaining * loads[i] // pool), rest)
            counts[i] = counts[i] + addition
            rest = rest - addition
    return np.array(counts)


def scatter_about(key, dims, spread, limit, shards=(), kind=jnp.bfloat16):
    level = block_levels(key, dims, shards, -0.22, 0.18) if shards else 1.0
    drawn = jax.random.normal(key, dims, jnp.float32) * spread * level
    return jnp.minimum(jnp.maximum(drawn, -limit), limit).astype(kind)


def setup_inputs(seed: int = 0) -> dict:
    key_list = jax.random.split(jax.random.key(seed), 11)
    amps = scatter_about(key_list[0], (PAIRS, VIRTUALS, VIRTUALS), 1.0, 6.0, ((0, 32),))
    rotation = scatter_about(key_list[1], (PAIRS, VIRTUALS, VIRTUALS), VIRTUALS ** -0.5, 0.5, ((0, 32),))
    intersections = scatter_about(key_list[2], (PAIRS, NEIGHBOURS, VIRTUALS, VIRTUALS), VIRTUALS ** -0.5, 0.5, ((0, 32),))
    energies = jnp.clip(jnp.exp(math.log(2.0) - 2.0794415 * jax.random.uniform(key_list[3], (PAIRS, VIRTUALS), jnp.float32) ** block_levels(key_list[3], (PAIRS, VIRTUALS), ((0, 32),), -0.2, 0.2)), 0.25, 2.0)
    domains = with_ends(jax.random.randint(key_list[4], (PAIRS, 2), 0, BLOCKS), jax.random.fold_in(key_list[4], 1), 0, BLOCKS - 1).astype(jnp.int32)
    owners_keys = jax.random.split(jax.random.fold_in(key_list[5], 1), PAIRS // PAIR_DEV)
    owners_turns = jax.random.permutation(jax.random.fold_in(key_list[5], 3), PAIRS // PAIR_DEV)
    owners = jax.vmap(lambda own, number: assign_block(jax.random.fold_in(key_list[5], 2), own, number, PAIR_DEV, N_PAIR, NEIGHBOURS, CAPACITY, 2))(owners_keys, owners_turns).reshape((PAIRS, NEIGHBOURS))
    slots = with_ends(jax.random.randint(key_list[6], (PAIRS, NEIGHBOURS), 0, PAIR_DEV), jax.random.fold_in(key_list[6], 1), 0, PAIR_DEV - 1).astype(jnp.int32)
    tiles = with_ends(jax.random.randint(key_list[7], (PAIRS,), 0, TILES), jax.random.fold_in(key_list[7], 1), 0, TILES - 1).astype(jnp.int32)
    blocks = scatter_about(key_list[8], (BLOCKS, AUX_FUNCS, VIRTUALS), 0.21, 3.0, ((0, 4),))
    coeffs = scatter_about(key_list[9], (TILES, VIRTUALS, AO_WIDTH), VIRTUALS ** -0.5, 0.5, ((0, 8), (2, 4)))
    return dict(amps=amps, rotation=rotation, intersections=intersections, energies=energies, domains=domains, owners=owners, slots=slots, tiles=tiles, blocks=blocks, coeffs=coeffs)


def reference(amps, rotation, intersections, energies, domains, owners, slots, tiles, blocks, coeffs):
    pairs = PAIR_DEV * N_PAIR * N_AUX
    groups = N_PAIR * N_AUX
    column = ((jnp.arange(pairs, dtype=jnp.int32) // PAIR_DEV) % N_AUX).astype(jnp.int32)
    target = ((owners * N_AUX + column[:, None]) * PAIR_DEV + slots).astype(jnp.int32)

    def grouped(value):
        return value.reshape((groups, PAIR_DEV) + value.shape[1:])

    def push_step(carry, inputs):
        amp_b, over_b, target_b = inputs
        half_push = jnp.einsum("pnba,pbc->pnac", over_b.astype(jnp.float32), amp_b.astype(jnp.float32)).astype(jnp.bfloat16)
        sent_blocks = jnp.einsum("pnac,pncd->pnad", half_push.astype(jnp.float32), over_b.astype(jnp.float32)).astype(jnp.bfloat16)
        carry = carry.at[target_b.reshape(-1)].add(sent_blocks.reshape(-1, VIRTUALS, VIRTUALS).astype(jnp.float32))
        return carry, None

    incoming_all, _ = lax.scan(push_step, jnp.zeros((pairs, VIRTUALS, VIRTUALS), jnp.float32),
                               (grouped(amps), grouped(intersections), grouped(target)))

    def update_step(carry, inputs):
        amp_b, rot_b, over_b, pair_energy_backward, domain_b, target_b, tile_b, incoming_b = inputs
        left_block = jnp.take(blocks, domain_b[:, 0], axis=0).astype(jnp.float32)
        right_density_block = jnp.take(blocks, domain_b[:, 1], axis=0).astype(jnp.float32)
        rot_f = rot_b.astype(jnp.float32)
        left_fit = jnp.einsum("pqa,pab->pqb", left_block, rot_f).astype(jnp.bfloat16)
        right_fit = jnp.einsum("pqa,pab->pqb", right_density_block, rot_f).astype(jnp.bfloat16)
        integrals = jnp.einsum("pqa,pqb->pab", left_fit.astype(jnp.float32), right_fit.astype(jnp.float32))
        partner = jnp.take(amps, target_b.reshape(-1), axis=0).reshape(PAIR_DEV, NEIGHBOURS, VIRTUALS, VIRTUALS)
        over_f = over_b.astype(jnp.float32)
        half_gathered = jnp.einsum("pnab,pnbc->pnac", over_f, partner.astype(jnp.float32)).astype(jnp.bfloat16)
        pulled = jnp.einsum("pnac,pndc->pad", half_gathered.astype(jnp.float32), over_f)
        denom = pair_energy_backward[:, :, None] + pair_energy_backward[:, None, :]
        amp_f = amp_b.astype(jnp.float32)
        residual = integrals + denom * amp_f - pulled - incoming_b
        new_b = (amp_f - residual / (denom + 1.0)).astype(jnp.bfloat16)
        new_f = new_b.astype(jnp.float32)
        pair_density = (jnp.einsum("pab,pcb->pac", new_f, new_f) * (1.0 / VIRTUALS)).astype(jnp.bfloat16)
        rotated = jnp.einsum("pab,pbc->pac", rot_f, pair_density.astype(jnp.float32)).astype(jnp.bfloat16)
        tile_density = jnp.einsum("pac,pdc->pad", rotated.astype(jnp.float32), rot_f)
        carry = carry.at[tile_b].add(tile_density)
        return carry, new_b

    tile_accumulated, new_blocks = lax.scan(update_step, jnp.zeros((TILES, VIRTUALS, VIRTUALS), jnp.float32),
                                    (grouped(amps), grouped(rotation), grouped(intersections), grouped(energies),
                                     grouped(domains), grouped(target), grouped(tiles), grouped(incoming_all)))
    new_amps = new_blocks.reshape(pairs, VIRTUALS, VIRTUALS)
    density = jnp.einsum("vsi,vik->vsk", tile_accumulated, coeffs.astype(jnp.float32),
                         precision=lax.Precision.HIGHEST) * (1.0 / (PAIR_DEV * N_AUX))
    return new_amps, density
```

```python
import functools

import jax
import jax.numpy as jnp
from jax import lax
from jax.experimental import pallas as pl
from jax.experimental.pallas import tpu as pltpu
from jax.sharding import PartitionSpec as P

MESH = pl.DeviceIdType.MESH
F32 = jnp.float32
BF16 = jnp.bfloat16


def mm(a, b, ca=1, cb=0):
    return lax.dot_general(a, b, (((ca,), (cb,)), ((), ())), preferred_element_type=F32)


def loop(lo, hi, body):
    def step(i, carry):
        body(i)
        return carry

    lax.fori_loop(lo, hi, step, 0)


def remote(src, dst, send, recv, **where):
    return pltpu.make_async_remote_copy(
        src_ref=src, dst_ref=dst, send_sem=send, recv_sem=recv, device_id=where, device_id_type=MESH
    )


def kernel(
    n, lines, n_aux, neighbours, factor,
    owners, slots, domains, tiles,
    amps, rotation, inter, energies, blocks, coeffs,
    new_amps, density,
    amps_all, blocks_all, push, sending, xrecv, hsum, zrecv, base, rcp, part, part_own, part_send, part_recv, tot_send, tot_recv,
    ag_send, ag_recv, fwd_send, blk_send, blk_recv, rx_send, rx_recv, rz_send, rz_recv,
    t_send, t_recv, a_send, a_recv,
):
    resident, width = amps.shape[0], amps.shape[1]
    owned = blocks.shape[0]
    held = coeffs.shape[0]
    me = lax.axis_index("pair")
    aux = lax.axis_index("aux")
    row, side = me // 2, me % 2
    mate = row * 2 + 1 - side

    barrier = pltpu.get_barrier_semaphore()

    def greet_pair(d):
        pl.semaphore_signal(barrier, inc=1, device_id={"pair": (me + d) % n}, device_id_type=MESH)

    def greet_aux(d):
        pl.semaphore_signal(barrier, inc=1, device_id={"aux": (aux + d) % n_aux}, device_id_type=MESH)

    loop(1, n, greet_pair)
    loop(1, n_aux, greet_aux)
    pl.semaphore_wait(barrier, n - 1 + n_aux - 1)

    def line_copy(d):
        return remote(
            amps, amps_all.at[pl.ds(me * resident, resident)], ag_send.at[d], ag_recv.at[me],
            pair=((row + d) % lines) * 2 + side,
        )

    mate_copy = remote(
        amps, amps_all.at[pl.ds(me * resident, resident)], ag_send.at[0], ag_recv.at[me], pair=mate
    )

    def block_copy(d):
        return remote(
            blocks, blocks_all.at[pl.ds(aux * owned, owned)], blk_send.at[d], blk_recv.at[aux],
            aux=(aux + d) % n_aux,
        )

    mate_copy.start()
    loop(1, lines, lambda d: line_copy(d).start())
    loop(1, n_aux, lambda d: block_copy(d).start())

    def keep(p):
        amps_all[me * resident + p] = amps[p]

    loop(0, resident, keep)

    def keep_block(j):
        blocks_all[aux * owned + j] = blocks[j]

    loop(0, owned, keep_block)

    def push_pair(p):
        own = amps[p]
        for k in range(neighbours):
            over = inter[p * neighbours + k]
            half = mm(over, own, 0, 0).astype(BF16)
            push[p * neighbours + k] = mm(half, over).astype(BF16)

    loop(0, resident, push_pair)

    chunk = 16

    def gathered(owner, emit):
        entry, slot = [], []
        for p in range(resident):
            e, s = p * neighbours, jnp.int32(-1)
            for k in range(neighbours):
                hit = owners[p * neighbours + k] == owner
                e = jnp.where(hit, p * neighbours + k, e)
                s = jnp.where(hit, slots[p * neighbours + k], s)
            entry.append(e)
            slot.append(s)
        weight = [
            [jnp.where(slot[p] == j, 1.0, 0.0).astype(F32) for p in range(resident)] for j in range(resident)
        ]

        def rows(c):
            at = pl.ds(pl.multiple_of(c * chunk, chunk), chunk)
            found = [push[entry[p], at, :].astype(F32) for p in range(resident)]
            for j in range(resident):
                total = weight[j][0] * found[0]
                for p in range(1, resident):
                    total = total + weight[j][p] * found[p]
                emit(j, at, total)

        loop(0, width // chunk, rows)

    def x_copy(h):
        return remote(sending.at[h], xrecv.at[h], rx_send.at[h], rx_recv.at[h], pair=mate)

    def x_send(d):
        h = (row + d) % lines

        def emit(j, at, total):
            sending[h, j, at, :] = total.astype(BF16)

        gathered(h * 2 + 1 - side, emit)
        x_copy(h).start()

    loop(1, lines + 1, x_send)

    def fwd_copy(h):
        src = amps_all.at[pl.ds((h * 2 + side) * resident, resident)]
        return remote(src, src, fwd_send.at[h], ag_recv.at[h * 2 + side], pair=mate)

    def arrived(src):
        here = amps_all.at[pl.ds(src * resident, resident)]
        remote(here, here, ag_send.at[0], ag_recv.at[src], pair=mate).wait_recv()

    def z_copy(d):
        h = (row + d) % lines
        return remote(hsum.at[h], zrecv.at[row], rz_send.at[h], rz_recv.at[row], pair=h * 2 + side)

    def second(d):
        h = (row + d) % lines
        arrived(h * 2 + side)
        fwd_copy(h).start()
        x_copy(h).wait_recv()

        def emit(j, at, total):
            hsum[h, j, at, :] = (total + xrecv[h, j, at, :].astype(F32)).astype(BF16)

        gathered(h * 2 + side, emit)
        z_copy(d).start()

    loop(1, lines, second)

    def block_arrived(d):
        src = (aux + d) % n_aux
        here = blocks_all.at[pl.ds(src * owned, owned)]
        remote(here, here, blk_send.at[0], blk_recv.at[src], aux=src).wait_recv()

    loop(1, n_aux, block_arrived)

    def integral(p):
        rot = rotation[p]
        left = mm(blocks_all[domains[2 * p]], rot).astype(BF16)
        right = mm(blocks_all[domains[2 * p + 1]], rot).astype(BF16)
        base[p] = mm(left, right, 0, 0)

    loop(0, resident, integral)

    loop(0, lines, lambda h: arrived(h * 2 + 1 - side))

    def pull_pair(p):
        total = base[p]
        for k in range(neighbours):
            over = inter[p * neighbours + k]
            at = owners[p * neighbours + k] * resident + slots[p * neighbours + k]
            half = mm(over, amps_all[at]).astype(BF16)
            total = total - mm(half, over, 1, 1)
        level = jnp.broadcast_to(energies[pl.ds(p, 1), :], (width, width))
        denom = level + level.T
        own = amps[p].astype(F32)
        inverse = 1.0 / (denom + 1.0)
        rcp[p] = inverse
        base[p] = own - (total + denom * own) * inverse

    loop(0, resident, pull_pair)

    x_copy(row).wait_recv()

    def emit_own(j, at, total):
        base[j, at, :] += (total + xrecv[row, j, at, :].astype(F32)) * rcp[j, at, :]

    gathered(me, emit_own)

    def z_arrived(d):
        h = (row + d) % lines
        here = zrecv.at[h]
        remote(here, here, rz_send.at[h], rz_recv.at[h], pair=h * 2 + side).wait_recv()

    loop(1, lines, z_arrived)

    def finish(p):
        incoming = zrecv[(row + 1) % lines, p].astype(F32)
        for d in range(2, lines):
            incoming = incoming + zrecv[(row + d) % lines, p].astype(F32)
        fresh = (base[p] + incoming * rcp[p]).astype(BF16)
        new_amps[p] = fresh
        rot = rotation[p]
        pair_density = (mm(fresh, fresh, 1, 1) * (1.0 / width)).astype(BF16)
        rotated = mm(rot, pair_density).astype(BF16)
        part[p] = mm(rotated, rot, 1, 1)

    loop(0, resident, finish)

    def t_copy(d):
        t = (me + d) % n
        return remote(part_send.at[t], part_recv.at[me], t_send.at[d], t_recv.at[me], pair=t)

    def tile_part(t, j):
        total = jnp.where(tiles[0] == t * held + j, 1.0, 0.0).astype(F32) * part[0]
        for p in range(1, resident):
            total = total + jnp.where(tiles[p] == t * held + j, 1.0, 0.0).astype(F32) * part[p]
        return total

    def tile_send(d):
        t = (me + d) % n
        for j in range(held):
            part_send[t, j] = tile_part(t, j).astype(BF16)
        t_copy(d).start()

    loop(1, n, tile_send)
    for j in range(held):
        part_own[j] = tile_part(me, j)

    def tile_add(d):
        src = (me + d) % n
        here = part_recv.at[src]
        remote(here, here, t_send.at[0], t_recv.at[src], pair=src).wait_recv()
        for j in range(held):
            part_own[j] += part_recv[src, j].astype(F32)

    loop(1, n, tile_add)
    tot_send[...] = part_own[...].astype(BF16)

    def a_copy(d):
        return remote(tot_send, tot_recv.at[aux], a_send.at[d], a_recv.at[aux], aux=(aux + d) % n_aux)

    loop(1, n_aux, lambda d: a_copy(d).start())

    def tot_add(d):
        src = (aux + d) % n_aux
        here = tot_recv.at[src]
        remote(here, here, a_send.at[0], a_recv.at[src], aux=src).wait_recv()
        for j in range(held):
            part_own[j] += tot_recv[src, j].astype(F32)

    loop(1, n_aux, tot_add)
    for j in range(held):
        total = part_own[j]
        high = total.astype(BF16)
        low = (total - high.astype(F32)).astype(BF16)
        density[j] = (mm(high, coeffs[j]) + mm(low, coeffs[j])) * factor

    mate_copy.wait_send()
    loop(1, lines, lambda d: line_copy(d).wait_send())
    loop(1, lines, lambda d: fwd_copy((row + d) % lines).wait_send())
    loop(1, lines, lambda d: z_copy(d).wait_send())
    loop(0, lines, lambda h: x_copy(h).wait_send())
    loop(1, n_aux, lambda d: block_copy(d).wait_send())
    loop(1, n, lambda d: t_copy(d).wait_send())
    loop(1, n_aux, lambda d: a_copy(d).wait_send())


def local(n, n_aux, amps, rotation, intersections, energies, domains, owners, slots, tiles, blocks, coeffs):
    resident, width = amps.shape[0], amps.shape[1]
    neighbours = owners.shape[1]
    entries = resident * neighbours
    lines = n // 2
    held = coeffs.shape[0]
    square = (width, width)
    dma = pltpu.SemaphoreType.DMA
    scratch = [
        ((n * resident,) + square, BF16),
        ((n_aux * blocks.shape[0],) + blocks.shape[1:], BF16),
        ((entries,) + square, BF16),
        ((lines, resident) + square, BF16),
        ((lines, resident) + square, BF16),
        ((lines, resident) + square, BF16),
        ((lines, resident) + square, BF16),
        ((resident,) + square, F32),
        ((resident,) + square, F32),
        ((resident,) + square, F32),
        ((held,) + square, F32),
        ((n, held) + square, BF16),
        ((n, held) + square, BF16),
        ((held,) + square, BF16),
        ((n_aux, held) + square, BF16),
    ]
    sems = [n, n, lines, n_aux, n_aux, lines, lines, lines, lines, n, n, n_aux, n_aux]
    smem = pl.BlockSpec(memory_space=pltpu.SMEM)
    vmem = pl.BlockSpec(memory_space=pltpu.VMEM)
    out_shape = (
        jax.ShapeDtypeStruct(amps.shape, BF16),
        jax.ShapeDtypeStruct((held, width, coeffs.shape[2]), F32),
    )
    size = 16 << 20
    for shape, kind in scratch:
        count = jnp.dtype(kind).itemsize
        for extent in shape:
            count *= extent
        size += count
    return pl.pallas_call(
        functools.partial(kernel, n, lines, n_aux, neighbours, 1.0 / (resident * n_aux)),
        out_shape=out_shape,
        in_specs=[smem] * 4 + [vmem] * 6,
        out_specs=(vmem, vmem),
        scratch_shapes=[pltpu.VMEM(*s) for s in scratch] + [dma((k,)) for k in sems],
        compiler_params=pltpu.CompilerParams(
            collective_id=0, has_side_effects=True, vmem_limit_bytes=min(size, 60 << 20)
        ),
    )(
        owners.reshape(entries),
        slots.reshape(entries),
        domains.reshape(2 * resident),
        tiles,
        amps,
        rotation,
        intersections.reshape((entries,) + square),
        energies,
        blocks,
        coeffs,
    )


def solution(mesh):
    return jax.shard_map(
        functools.partial(local, mesh.shape["pair"], mesh.shape["aux"]),
        mesh=mesh,
        in_specs=(
            P(("pair", "aux"), None, None),
            P(("pair", "aux"), None, None),
            P(("pair", "aux"), None, None, None),
            P(("pair", "aux"), None),
            P(("pair", "aux"), None),
            P(("pair", "aux"), None),
            P(("pair", "aux"), None),
            P(("pair", "aux")),
            P("aux", None, None),
            P("pair", None, "aux"),
        ),
        out_specs=(P(("pair", "aux"), None, None), P("pair", None, "aux")),
        check_vma=False,
    )
```

```python
import functools

import jax
import jax.numpy as jnp
from jax import lax
from jax.experimental import pallas as pl
from jax.experimental.pallas import tpu as pltpu
from jax.sharding import PartitionSpec as P

MESH = pl.DeviceIdType.MESH
F32 = jnp.float32
BF16 = jnp.bfloat16


def mm(a, b, ca=1, cb=0):
    return lax.dot_general(a, b, (((ca,), (cb,)), ((), ())), preferred_element_type=F32)


def loop(lo, hi, body):
    def step(i, carry):
        body(i)
        return carry

    lax.fori_loop(lo, hi, step, 0)


def remote(src, dst, send, recv, **where):
    return pltpu.make_async_remote_copy(
        src_ref=src, dst_ref=dst, send_sem=send, recv_sem=recv, device_id=where, device_id_type=MESH
    )


def kernel(
    n, lines, n_aux, neighbours, factor,
    owners_in, slots_in, domains_in, tiles_in,
    amps_in, rotation_in, inter_in, energies_in, blocks_in, coeffs_in,
    new_amps, density,
    owners, slots, domains, tiles, rotation, inter, energies, coeffs,
    amps_all, blocks_all, push, sending, xrecv, hsum, zrecv, base, rcp, part, part_own, part_send, part_recv, tot_send, tot_recv,
    in_sem, up_send, down_send, ag_recv, fwd_send, blk_send, blk_recv, rx_send, rx_recv, rz_send, rz_recv,
    t_send, t_recv, a_send, a_recv,
):
    resident, width = amps_in.shape[0], amps_in.shape[1]
    owned = blocks_in.shape[0]
    held = coeffs_in.shape[0]
    me = lax.axis_index("pair")
    aux = lax.axis_index("aux")
    row, side = me // 2, me % 2
    mate = row * 2 + 1 - side

    def rows_of(src):
        return amps_all.at[pl.ds(src * resident, resident)]

    staged = [
        pltpu.make_async_copy(src, dst, in_sem.at[i])
        for i, (src, dst) in enumerate([
            (amps_in, rows_of(me)),
            (blocks_in, blocks_all.at[pl.ds(aux * owned, owned)]),
            (inter_in, inter),
            (owners_in, owners),
            (slots_in, slots),
            (domains_in, domains),
            (tiles_in, tiles),
            (energies_in, energies),
            (rotation_in, rotation),
            (coeffs_in, coeffs),
        ])
    ]
    for copy in staged:
        copy.start()

    barrier = pltpu.get_barrier_semaphore()

    def greet_pair(d):
        pl.semaphore_signal(barrier, inc=1, device_id={"pair": (me + d) % n}, device_id_type=MESH)

    def greet_aux(d):
        pl.semaphore_signal(barrier, inc=1, device_id={"aux": (aux + d) % n_aux}, device_id_type=MESH)

    loop(1, n, greet_pair)
    loop(1, n_aux, greet_aux)
    staged[0].wait()
    staged[1].wait()
    pl.semaphore_wait(barrier, n - 1 + n_aux - 1)

    def own_row(h):
        return h * 2 + side

    def up_copy(h):
        src = rows_of(own_row(h))
        return remote(src, src, up_send.at[h], ag_recv.at[own_row(h)], pair=me + 2)

    def down_copy(h):
        src = rows_of(own_row(h))
        return remote(src, src, down_send.at[h], ag_recv.at[own_row(h)], pair=me - 2)

    def fwd_copy(h):
        src = rows_of(own_row(h))
        return remote(src, src, fwd_send.at[h], ag_recv.at[own_row(h)], pair=mate)

    def arrived(src):
        here = rows_of(src)
        remote(here, here, fwd_send.at[0], ag_recv.at[src], pair=mate).wait_recv()

    def block_copy(d):
        here = blocks_all.at[pl.ds(aux * owned, owned)]
        return remote(here, here, blk_send.at[d], blk_recv.at[aux], aux=(aux + d) % n_aux)

    @pl.when(row + 1 < lines)
    def _():
        up_copy(row).start()

    @pl.when(row > 0)
    def _():
        down_copy(row).start()

    fwd_copy(row).start()
    loop(1, n_aux, lambda d: block_copy(d).start())

    def line_step(s):
        @pl.when(row - s >= 0)
        def _():
            arrived(own_row(row - s))

            @pl.when(row + 1 < lines)
            def _():
                up_copy(row - s).start()

            fwd_copy(row - s).start()

        @pl.when(row + s < lines)
        def _():
            arrived(own_row(row + s))

            @pl.when(row > 0)
            def _():
                down_copy(row + s).start()

            fwd_copy(row + s).start()

    for copy in staged[2:]:
        copy.wait()

    def push_pair(p):
        own = amps_all[me * resident + p]
        for k in range(neighbours):
            over = inter[p * neighbours + k]
            half = mm(over, own, 0, 0).astype(BF16)
            push[p * neighbours + k] = mm(half, over).astype(BF16)

    loop(0, resident, push_pair)

    chunk = 16

    def gathered(owner, emit):
        entry, slot = [], []
        for p in range(resident):
            e, s = p * neighbours, jnp.int32(-1)
            for k in range(neighbours):
                hit = owners[p, k] == owner
                e = jnp.where(hit, p * neighbours + k, e)
                s = jnp.where(hit, slots[p, k], s)
            entry.append(e)
            slot.append(s)
        weight = [
            [jnp.where(slot[p] == j, 1.0, 0.0).astype(F32) for p in range(resident)] for j in range(resident)
        ]

        def rows(c):
            at = pl.ds(pl.multiple_of(c * chunk, chunk), chunk)
            found = [push[entry[p], at, :].astype(F32) for p in range(resident)]
            for j in range(resident):
                total = weight[j][0] * found[0]
                for p in range(1, resident):
                    total = total + weight[j][p] * found[p]
                emit(j, at, total)

        loop(0, width // chunk, rows)

    def x_copy(h):
        return remote(sending.at[h], xrecv.at[h], rx_send.at[h], rx_recv.at[h], pair=mate)

    def x_send(d):
        h = (row + d) % lines

        def emit(j, at, total):
            sending[h, j, at, :] = total.astype(BF16)

        gathered(h * 2 + 1 - side, emit)
        x_copy(h).start()

    def turn(s):
        return (s + lines // 2 - 2) % (lines - 1) + 1

    def first(s):
        x_send(turn(s))
        line_step(s)

    loop(1, lines, first)
    x_send(lines)

    def z_copy(d):
        h = (row + d) % lines
        return remote(hsum.at[h], zrecv.at[row], rz_send.at[h], rz_recv.at[row], pair=h * 2 + side)

    def second(s):
        d = turn(s)
        h = (row + d) % lines
        x_copy(h).wait_recv()

        def emit(j, at, total):
            hsum[h, j, at, :] = (total + xrecv[h, j, at, :].astype(F32)).astype(BF16)

        gathered(h * 2 + side, emit)
        z_copy(d).start()

    def block_arrived(d):
        src = (aux + d) % n_aux
        here = blocks_all.at[pl.ds(src * owned, owned)]
        remote(here, here, blk_send.at[0], blk_recv.at[src], aux=src).wait_recv()

    loop(1, n_aux, block_arrived)

    def integral(p):
        rot = rotation[p]
        left = mm(blocks_all[domains[p, 0]], rot).astype(BF16)
        right = mm(blocks_all[domains[p, 1]], rot).astype(BF16)
        base[p] = mm(left, right, 0, 0)

    second(1)
    loop(0, resident, integral)
    loop(2, lines, second)

    loop(0, lines, lambda h: arrived(h * 2 + 1 - side))

    def pull_pair(p):
        total = base[p]
        for k in range(neighbours):
            over = inter[p * neighbours + k]
            at = owners[p, k] * resident + slots[p, k]
            half = mm(over, amps_all[at]).astype(BF16)
            total = total - mm(half, over, 1, 1)
        level = jnp.broadcast_to(energies[pl.ds(p, 1), :], (width, width))
        denom = level + level.T
        own = amps_all[me * resident + p].astype(F32)
        inverse = 1.0 / (denom + 1.0)
        rcp[p] = inverse
        base[p] = own - (total + denom * own) * inverse

    loop(0, resident, pull_pair)

    x_copy(row).wait_recv()

    def emit_own(j, at, total):
        base[j, at, :] += (total + xrecv[row, j, at, :].astype(F32)) * rcp[j, at, :]

    gathered(me, emit_own)

    def z_arrived(d):
        h = (row + d) % lines
        here = zrecv.at[h]
        remote(here, here, rz_send.at[h], rz_recv.at[h], pair=h * 2 + side).wait_recv()

    loop(1, lines, z_arrived)

    def finish(p):
        incoming = zrecv[(row + 1) % lines, p].astype(F32)
        for d in range(2, lines):
            incoming = incoming + zrecv[(row + d) % lines, p].astype(F32)
        fresh = (base[p] + incoming * rcp[p]).astype(BF16)
        new_amps[p] = fresh
        rot = rotation[p]
        pair_density = (mm(fresh, fresh, 1, 1) * (1.0 / width)).astype(BF16)
        rotated = mm(rot, pair_density).astype(BF16)
        part[p] = mm(rotated, rot, 1, 1)

    loop(0, resident, finish)

    def t_copy(d):
        t = (me + d) % n
        return remote(part_send.at[t], part_recv.at[me], t_send.at[d], t_recv.at[me], pair=t)

    def tile_part(t, j):
        total = jnp.where(tiles[0] == t * held + j, 1.0, 0.0).astype(F32) * part[0]
        for p in range(1, resident):
            total = total + jnp.where(tiles[p] == t * held + j, 1.0, 0.0).astype(F32) * part[p]
        return total

    def tile_send(d):
        t = (me + d) % n
        for j in range(held):
            part_send[t, j] = tile_part(t, j).astype(BF16)
        t_copy(d).start()

    loop(1, n, tile_send)
    for j in range(held):
        part_own[j] = tile_part(me, j)

    def tile_add(d):
        src = (me + d) % n
        here = part_recv.at[src]
        remote(here, here, t_send.at[0], t_recv.at[src], pair=src).wait_recv()
        for j in range(held):
            part_own[j] += part_recv[src, j].astype(F32)

    loop(1, n, tile_add)
    tot_send[...] = part_own[...].astype(BF16)

    def a_copy(d):
        return remote(tot_send, tot_recv.at[aux], a_send.at[d], a_recv.at[aux], aux=(aux + d) % n_aux)

    loop(1, n_aux, lambda d: a_copy(d).start())

    def tot_add(d):
        src = (aux + d) % n_aux
        here = tot_recv.at[src]
        remote(here, here, a_send.at[0], a_recv.at[src], aux=src).wait_recv()
        for j in range(held):
            part_own[j] += tot_recv[src, j].astype(F32)

    loop(1, n_aux, tot_add)
    for j in range(held):
        total = part_own[j]
        high = total.astype(BF16)
        low = (total - high.astype(F32)).astype(BF16)
        density[j] = (mm(high, coeffs[j]) + mm(low, coeffs[j])) * factor

    def line_left(h):
        @pl.when((row + 1 < lines) & (h <= row))
        def _():
            up_copy(h).wait_send()

        @pl.when((row > 0) & (h >= row))
        def _():
            down_copy(h).wait_send()

        fwd_copy(h).wait_send()

    loop(0, lines, line_left)
    loop(1, lines, lambda d: z_copy(d).wait_send())
    loop(0, lines, lambda h: x_copy(h).wait_send())
    loop(1, n_aux, lambda d: block_copy(d).wait_send())
    loop(1, n, lambda d: t_copy(d).wait_send())
    loop(1, n_aux, lambda d: a_copy(d).wait_send())


def local(n, n_aux, amps, rotation, intersections, energies, domains, owners, slots, tiles, blocks, coeffs):
    resident, width = amps.shape[0], amps.shape[1]
    neighbours = owners.shape[1]
    entries = resident * neighbours
    lines = n // 2
    held = coeffs.shape[0]
    square = (width, width)
    dma = pltpu.SemaphoreType.DMA
    scratch = [
        (rotation.shape, BF16),
        ((entries,) + square, BF16),
        (energies.shape, F32),
        (coeffs.shape, BF16),
        ((n * resident,) + square, BF16),
        ((n_aux * blocks.shape[0],) + blocks.shape[1:], BF16),
        ((entries,) + square, BF16),
        ((lines, resident) + square, BF16),
        ((lines, resident) + square, BF16),
        ((lines, resident) + square, BF16),
        ((lines, resident) + square, BF16),
        ((resident,) + square, F32),
        ((resident,) + square, F32),
        ((resident,) + square, F32),
        ((held,) + square, F32),
        ((n, held) + square, BF16),
        ((n, held) + square, BF16),
        ((held,) + square, BF16),
        ((n_aux, held) + square, BF16),
    ]
    sems = [10, lines, lines, n, lines, n_aux, n_aux, lines, lines, lines, lines, n, n, n_aux, n_aux]
    hbm = pl.BlockSpec(memory_space=pltpu.HBM)
    vmem = pl.BlockSpec(memory_space=pltpu.VMEM)
    out_shape = (
        jax.ShapeDtypeStruct(amps.shape, BF16),
        jax.ShapeDtypeStruct((held, width, coeffs.shape[2]), F32),
    )
    return pl.pallas_call(
        functools.partial(kernel, n, lines, n_aux, neighbours, 1.0 / (resident * n_aux)),
        out_shape=out_shape,
        in_specs=[hbm] * 10,
        out_specs=(vmem, vmem),
        scratch_shapes=[pltpu.SMEM(x.shape, jnp.int32) for x in (owners, slots, domains, tiles)]
        + [pltpu.VMEM(*s) for s in scratch]
        + [dma((k,)) for k in sems],
        compiler_params=pltpu.CompilerParams(
            collective_id=0, has_side_effects=True, vmem_limit_bytes=60 << 20
        ),
    )(
        owners,
        slots,
        domains,
        tiles,
        amps,
        rotation,
        intersections.reshape((entries,) + square),
        energies,
        blocks,
        coeffs,
    )


def solution(mesh):
    return jax.shard_map(
        functools.partial(local, mesh.shape["pair"], mesh.shape["aux"]),
        mesh=mesh,
        in_specs=(
            P(("pair", "aux"), None, None),
            P(("pair", "aux"), None, None),
            P(("pair", "aux"), None, None, None),
            P(("pair", "aux"), None),
            P(("pair", "aux"), None),
            P(("pair", "aux"), None),
            P(("pair", "aux"), None),
            P(("pair", "aux")),
            P("aux", None, None),
            P("pair", None, "aux"),
        ),
        out_specs=(P(("pair", "aux"), None, None), P("pair", None, "aux")),
        check_vma=False,
    )
```

```python
import functools

import jax
import jax.numpy as jnp
from jax import lax
from jax.experimental import pallas as pl
from jax.experimental.pallas import tpu as pltpu
from jax.sharding import PartitionSpec as P

MESH = pl.DeviceIdType.MESH
F32 = jnp.float32
BF16 = jnp.bfloat16


def mm(a, b, ca=1, cb=0):
    return lax.dot_general(a, b, (((ca,), (cb,)), ((), ())), preferred_element_type=F32)


def loop(lo, hi, body):
    def step(i, carry):
        body(i)
        return carry

    lax.fori_loop(lo, hi, step, 0)


def remote(src, dst, send, recv, **where):
    return pltpu.make_async_remote_copy(
        src_ref=src, dst_ref=dst, send_sem=send, recv_sem=recv, device_id=where, device_id_type=MESH
    )


def kernel(
    n, lines, n_aux, neighbours, factor,
    owners_in, slots_in, domains_in, tiles_in,
    amps_in, rotation_in, inter_in, energies_in, blocks_in, coeffs_in,
    new_amps, density,
    owners, slots, domains, tiles, rotation, inter, energies, coeffs,
    amps_all, blocks_all, push, sending, xrecv, hsum, zrecv, base, rcp, part, part_own, part_send, part_recv, tot_send, tot_recv,
    in_sem, up_send, down_send, ag_recv, fwd_send, blk_send, blk_recv, rx_send, rx_recv, rz_send, rz_recv,
    t_send, t_recv, a_send, a_recv,
):
    resident, width = amps_in.shape[0], amps_in.shape[1]
    owned = blocks_in.shape[0]
    held = coeffs_in.shape[0]
    me = lax.axis_index("pair")
    aux = lax.axis_index("aux")
    row, side = me // 2, me % 2
    mate = row * 2 + 1 - side

    def rows_of(src):
        return amps_all.at[pl.ds(src * resident, resident)]

    staged = [
        pltpu.make_async_copy(src, dst, in_sem.at[i])
        for i, (src, dst) in enumerate([
            (amps_in, rows_of(me)),
            (blocks_in, blocks_all.at[pl.ds(aux * owned, owned)]),
            (inter_in, inter),
            (owners_in, owners),
            (slots_in, slots),
            (domains_in, domains),
            (tiles_in, tiles),
            (energies_in, energies),
            (rotation_in, rotation),
            (coeffs_in, coeffs),
        ])
    ]
    for copy in staged:
        copy.start()

    barrier = pltpu.get_barrier_semaphore()

    def greet_pair(d):
        pl.semaphore_signal(barrier, inc=1, device_id={"pair": (me + d) % n}, device_id_type=MESH)

    def greet_aux(d):
        pl.semaphore_signal(barrier, inc=1, device_id={"aux": (aux + d) % n_aux}, device_id_type=MESH)

    loop(1, n, greet_pair)
    loop(1, n_aux, greet_aux)
    staged[0].wait()
    staged[1].wait()
    pl.semaphore_wait(barrier, n - 1 + n_aux - 1)

    def own_row(h):
        return h * 2 + side

    def up_copy(h):
        src = rows_of(own_row(h))
        return remote(src, src, up_send.at[h], ag_recv.at[own_row(h)], pair=me + 2)

    def down_copy(h):
        src = rows_of(own_row(h))
        return remote(src, src, down_send.at[h], ag_recv.at[own_row(h)], pair=me - 2)

    def fwd_copy(h):
        src = rows_of(own_row(h))
        return remote(src, src, fwd_send.at[h], ag_recv.at[own_row(h)], pair=mate)

    def arrived(src):
        here = rows_of(src)
        remote(here, here, fwd_send.at[0], ag_recv.at[src], pair=mate).wait_recv()

    def block_copy(d):
        here = blocks_all.at[pl.ds(aux * owned, owned)]
        return remote(here, here, blk_send.at[d], blk_recv.at[aux], aux=(aux + d) % n_aux)

    @pl.when(row + 1 < lines)
    def _():
        up_copy(row).start()

    @pl.when(row > 0)
    def _():
        down_copy(row).start()

    fwd_copy(row).start()
    loop(1, n_aux, lambda d: block_copy(d).start())

    def line_step(s):
        @pl.when(row - s >= 0)
        def _():
            arrived(own_row(row - s))

            @pl.when(row + 1 < lines)
            def _():
                up_copy(row - s).start()

            fwd_copy(row - s).start()

        @pl.when(row + s < lines)
        def _():
            arrived(own_row(row + s))

            @pl.when(row > 0)
            def _():
                down_copy(row + s).start()

            fwd_copy(row + s).start()

    for copy in staged[2:]:
        copy.wait()

    group = 4 if resident % 4 == 0 else 1
    some = range(group)

    def push_pairs(i):
        for p in (2 * i, 2 * i + 1):
            own = amps_all[me * resident + p]
            over = [inter[p * neighbours + k] for k in range(neighbours)]
            half = [mm(x, own, 0, 0).astype(BF16) for x in over]
            for k in range(neighbours):
                push[p * neighbours + k] = mm(half[k], over[k]).astype(BF16)

    loop(0, resident // 2, push_pairs)

    chunk = 16

    half_slots = resident // 2

    def gathered(owner, part_at, emit):
        entry, slot = [], []
        for p in range(resident):
            e, s = p * neighbours, jnp.int32(-1)
            for k in range(neighbours):
                hit = owners[k, p] == owner
                e = jnp.where(hit, p * neighbours + k, e)
                s = jnp.where(hit, slots[k, p], s)
            entry.append(e)
            slot.append(s)
        weight = [
            [jnp.where(slot[p] == part_at * half_slots + j, 1.0, 0.0).astype(F32) for p in range(resident)]
            for j in range(half_slots)
        ]

        def rows(c):
            at = pl.ds(pl.multiple_of(c * chunk, chunk), chunk)
            found = [push[entry[p], at, :].astype(F32) for p in range(resident)]
            for j in range(half_slots):
                total = weight[j][0] * found[0]
                for p in range(1, resident):
                    total = total + weight[j][p] * found[p]
                emit(part_at * half_slots + j, at, total)

        loop(0, width // chunk, rows)

    def half_of(ref, h, q):
        return ref.at[h, pl.ds(q * half_slots, half_slots)]

    def x_copy(h, q):
        return remote(half_of(sending, h, q), half_of(xrecv, h, q), rx_send.at[h, q], rx_recv.at[h, q], pair=mate)

    def x_send(d, q):
        h = (row + d) % lines

        def emit(j, at, total):
            sending[h, j, at, :] = total.astype(BF16)

        gathered(h * 2 + 1 - side, q, emit)
        x_copy(h, q).start()

    def turn(s):
        return (s + lines // 2 - 2) % (lines - 1) + 1

    def first(s):
        x_send(turn(s), 0)
        line_step(s)

    loop(1, lines, first)
    x_send(lines, 0)
    loop(1, lines, lambda s: x_send(turn(s), 1))
    x_send(lines, 1)

    def z_copy(d, q):
        h = (row + d) % lines
        return remote(
            half_of(hsum, h, q), half_of(zrecv, row, q), rz_send.at[h, q], rz_recv.at[row, q], pair=h * 2 + side
        )

    def second(s, q):
        d = turn(s)
        h = (row + d) % lines
        x_copy(h, q).wait_recv()

        def emit(j, at, total):
            hsum[h, j, at, :] = (total + xrecv[h, j, at, :].astype(F32)).astype(BF16)

        gathered(h * 2 + side, q, emit)
        z_copy(d, q).start()

    def block_arrived(d):
        src = (aux + d) % n_aux
        here = blocks_all.at[pl.ds(src * owned, owned)]
        remote(here, here, blk_send.at[0], blk_recv.at[src], aux=src).wait_recv()

    loop(1, n_aux, block_arrived)

    def integral(i):
        pairs = [i * group + g for g in some]
        rot = [rotation[p] for p in pairs]
        gram = [mm(blocks_all[domains[0, p]], blocks_all[domains[1, p]], 0, 0).astype(BF16) for p in pairs]
        right = [mm(gram[g], rot[g]).astype(BF16) for g in some]
        for g in some:
            base[pairs[g]] = mm(rot[g], right[g], 0, 0)

    loop(0, resident // group, integral)
    loop(1, lines, lambda s: second(s, 0))

    loop(0, lines, lambda h: arrived(h * 2 + 1 - side))

    def pull_pairs(i):
        for p in (2 * i, 2 * i + 1):
            over = [inter[p * neighbours + k] for k in range(neighbours)]
            half = [
                mm(over[k], amps_all[owners[k, p] * resident + slots[k, p]]).astype(BF16) for k in range(neighbours)
            ]
            total = base[p]
            for k in range(neighbours):
                total = total - mm(half[k], over[k], 1, 1)
            level = jnp.broadcast_to(energies[pl.ds(p, 1), :], (width, width))
            denom = level + level.T
            own = amps_all[me * resident + p].astype(F32)
            inverse = 1.0 / (denom + 1.0)
            rcp[p] = inverse
            base[p] = own - (total + denom * own) * inverse

    loop(0, resident // 2, pull_pairs)

    def own_part(q):
        x_copy(row, q).wait_recv()

        def emit_own(j, at, total):
            base[j, at, :] += (total + xrecv[row, j, at, :].astype(F32)) * rcp[j, at, :]

        gathered(me, q, emit_own)

    def z_arrived(d, q):
        h = (row + d) % lines
        here = half_of(zrecv, h, q)
        remote(here, here, rz_send.at[h, q], rz_recv.at[h, q], pair=h * 2 + side).wait_recv()

    def finish(q):
        pairs = [q * half_slots + g for g in range(half_slots)]
        fresh = []
        for p in pairs:
            incoming = zrecv[(row + 1) % lines, p].astype(F32)
            for d in range(2, lines):
                incoming = incoming + zrecv[(row + d) % lines, p].astype(F32)
            fresh.append((base[p] + incoming * rcp[p]).astype(BF16))
            new_amps[p] = fresh[-1]
        rot = [rotation[p] for p in pairs]
        pair_density = [(mm(x, x, 1, 1) * (1.0 / width)).astype(BF16) for x in fresh]
        rotated = [mm(r, x).astype(BF16) for r, x in zip(rot, pair_density)]
        for p, r, x in zip(pairs, rot, rotated):
            part[p] = mm(x, r, 1, 1)

    def last(q):
        own_part(q)
        loop(1, lines, lambda d: z_arrived(d, q))
        finish(q)

    loop(1, lines, lambda s: second(s, 1))
    loop(0, 2, last)

    def t_copy(d):
        t = (me + d) % n
        return remote(part_send.at[t], part_recv.at[me], t_send.at[d], t_recv.at[me], pair=t)

    def tile_part(t, j):
        total = jnp.where(tiles[0] == t * held + j, 1.0, 0.0).astype(F32) * part[0]
        for p in range(1, resident):
            total = total + jnp.where(tiles[p] == t * held + j, 1.0, 0.0).astype(F32) * part[p]
        return total

    def tile_send(d):
        t = (me + d) % n
        for j in range(held):
            part_send[t, j] = tile_part(t, j).astype(BF16)
        t_copy(d).start()

    loop(1, n, tile_send)
    for j in range(held):
        part_own[j] = tile_part(me, j)

    def tile_add(d):
        src = (me + d) % n
        here = part_recv.at[src]
        remote(here, here, t_send.at[0], t_recv.at[src], pair=src).wait_recv()
        for j in range(held):
            part_own[j] += part_recv[src, j].astype(F32)

    loop(1, n, tile_add)
    tot_send[...] = part_own[...].astype(BF16)

    def a_copy(d):
        return remote(tot_send, tot_recv.at[aux], a_send.at[d], a_recv.at[aux], aux=(aux + d) % n_aux)

    loop(1, n_aux, lambda d: a_copy(d).start())

    def tot_add(d):
        src = (aux + d) % n_aux
        here = tot_recv.at[src]
        remote(here, here, a_send.at[0], a_recv.at[src], aux=src).wait_recv()
        for j in range(held):
            part_own[j] += tot_recv[src, j].astype(F32)

    loop(1, n_aux, tot_add)
    for j in range(held):
        total = part_own[j]
        high = total.astype(BF16)
        low = (total - high.astype(F32)).astype(BF16)
        density[j] = (mm(high, coeffs[j]) + mm(low, coeffs[j])) * factor

    def line_left(h):
        @pl.when((row + 1 < lines) & (h <= row))
        def _():
            up_copy(h).wait_send()

        @pl.when((row > 0) & (h >= row))
        def _():
            down_copy(h).wait_send()

        fwd_copy(h).wait_send()

    loop(0, lines, line_left)
    for q in range(2):
        loop(1, lines, lambda d: z_copy(d, q).wait_send())
        loop(0, lines, lambda h: x_copy(h, q).wait_send())
    loop(1, n_aux, lambda d: block_copy(d).wait_send())
    loop(1, n, lambda d: t_copy(d).wait_send())
    loop(1, n_aux, lambda d: a_copy(d).wait_send())


def local(n, n_aux, amps, rotation, intersections, energies, domains, owners, slots, tiles, blocks, coeffs):
    resident, width = amps.shape[0], amps.shape[1]
    neighbours = owners.shape[1]
    entries = resident * neighbours
    lines = n // 2
    held = coeffs.shape[0]
    square = (width, width)
    dma = pltpu.SemaphoreType.DMA
    scratch = [
        (rotation.shape, BF16),
        ((entries,) + square, BF16),
        (energies.shape, F32),
        (coeffs.shape, BF16),
        ((n * resident,) + square, BF16),
        ((n_aux * blocks.shape[0],) + blocks.shape[1:], BF16),
        ((entries,) + square, BF16),
        ((lines, resident) + square, BF16),
        ((lines, resident) + square, BF16),
        ((lines, resident) + square, BF16),
        ((lines, resident) + square, BF16),
        ((resident,) + square, F32),
        ((resident,) + square, F32),
        ((resident,) + square, F32),
        ((held,) + square, F32),
        ((n, held) + square, BF16),
        ((n, held) + square, BF16),
        ((held,) + square, BF16),
        ((n_aux, held) + square, BF16),
    ]
    halves = (lines, 2)
    sems = [10, lines, lines, n, lines, n_aux, n_aux, halves, halves, halves, halves, n, n, n_aux, n_aux]
    hbm = pl.BlockSpec(memory_space=pltpu.HBM)
    vmem = pl.BlockSpec(memory_space=pltpu.VMEM)
    out_shape = (
        jax.ShapeDtypeStruct(amps.shape, BF16),
        jax.ShapeDtypeStruct((held, width, coeffs.shape[2]), F32),
    )
    return pl.pallas_call(
        functools.partial(kernel, n, lines, n_aux, neighbours, 1.0 / (resident * n_aux)),
        out_shape=out_shape,
        in_specs=[hbm] * 10,
        out_specs=(vmem, vmem),
        scratch_shapes=[pltpu.SMEM(x.shape, jnp.int32) for x in (owners.T, slots.T, domains.T, tiles)]
        + [pltpu.VMEM(*s) for s in scratch]
        + [dma(k if isinstance(k, tuple) else (k,)) for k in sems],
        compiler_params=pltpu.CompilerParams(
            collective_id=0, has_side_effects=True, vmem_limit_bytes=60 << 20
        ),
    )(
        owners.T,
        slots.T,
        domains.T,
        tiles,
        amps,
        rotation,
        intersections.reshape((entries,) + square),
        energies,
        blocks,
        coeffs,
    )


def solution(mesh):
    return jax.shard_map(
        functools.partial(local, mesh.shape["pair"], mesh.shape["aux"]),
        mesh=mesh,
        in_specs=(
            P(("pair", "aux"), None, None),
            P(("pair", "aux"), None, None),
            P(("pair", "aux"), None, None, None),
            P(("pair", "aux"), None),
            P(("pair", "aux"), None),
            P(("pair", "aux"), None),
            P(("pair", "aux"), None),
            P(("pair", "aux")),
            P("aux", None, None),
            P("pair", None, "aux"),
        ),
        out_specs=(P(("pair", "aux"), None, None), P("pair", None, "aux")),
        check_vma=False,
    )
```

```python
import functools

import jax
import jax.numpy as jnp
from jax import lax
from jax.experimental import pallas as pl
from jax.experimental.pallas import tpu as pltpu
from jax.sharding import PartitionSpec as P

MESH = pl.DeviceIdType.MESH
F32 = jnp.float32
BF16 = jnp.bfloat16


def mm(a, b, ca=1, cb=0):
    return lax.dot_general(a, b, (((ca,), (cb,)), ((), ())), preferred_element_type=F32)


def loop(lo, hi, body):
    def step(i, carry):
        body(i)
        return carry

    lax.fori_loop(lo, hi, step, 0)


def remote(src, dst, send, recv, **where):
    return pltpu.make_async_remote_copy(
        src_ref=src, dst_ref=dst, send_sem=send, recv_sem=recv, device_id=where, device_id_type=MESH
    )


def kernel(
    n, lines, n_aux, neighbours, factor,
    owners_in, slots_in, domains_in, tiles_in,
    amps_in, rotation_in, inter_in, energies_in, blocks_in, coeffs_in,
    new_amps, density,
    owners, slots, domains, tiles, rotation, inter, energies, coeffs,
    amps_all, blocks_all, push, sending, xrecv, zsend, zrecv, last_send, last_recv,
    base, rcp, part, part_own, part_send, part_recv, tot_send, tot_recv,
    in_sem, up_send, down_send, ag_recv, up_late, down_late, late_recv, fwd_send, fwd_recv, blk_send, blk_recv,
    rx_send, rx_recv, rz_send, rz_recv, last_sems,
    t_send, t_recv, a_send, a_recv,
):
    resident, width = amps_in.shape[0], amps_in.shape[1]
    owned = blocks_in.shape[0]
    held = coeffs_in.shape[0]
    me = lax.axis_index("pair")
    aux = lax.axis_index("aux")
    row, side = me // 2, me % 2
    mate = row * 2 + 1 - side

    def rows_of(src):
        return amps_all.at[pl.ds(src * resident, resident)]

    staged = [
        pltpu.make_async_copy(src, dst, in_sem.at[i])
        for i, (src, dst) in enumerate([
            (amps_in, rows_of(me)),
            (blocks_in, blocks_all.at[pl.ds(aux * owned, owned)]),
            (inter_in, inter),
            (owners_in, owners),
            (slots_in, slots),
            (domains_in, domains),
            (tiles_in, tiles),
            (energies_in, energies),
            (rotation_in, rotation),
            (coeffs_in, coeffs),
        ])
    ]
    for copy in staged:
        copy.start()

    barrier = pltpu.get_barrier_semaphore()

    def greet_pair(d):
        pl.semaphore_signal(barrier, inc=1, device_id={"pair": (me + d) % n}, device_id_type=MESH)

    def greet_aux(d):
        pl.semaphore_signal(barrier, inc=1, device_id={"aux": (aux + d) % n_aux}, device_id_type=MESH)

    loop(1, n, greet_pair)
    loop(1, n_aux, greet_aux)
    staged[0].wait()
    staged[1].wait()
    pl.semaphore_wait(barrier, n - 1 + n_aux - 1)

    half_slots = resident // 2

    def own_row(h):
        return rows_of(h * 2 + side)

    def half_row(h, column, q):
        return amps_all.at[pl.ds((h * 2 + column) * resident + q * half_slots, half_slots)]

    def up_copy(h):
        return remote(own_row(h), own_row(h), up_send.at[h], ag_recv.at[h], pair=me + 2)

    def down_copy(h):
        return remote(own_row(h), own_row(h), down_send.at[h], ag_recv.at[h], pair=me - 2)

    def up_late_copy(h):
        src = half_row(h, 1 - side, 1)
        return remote(src, src, up_late.at[h], late_recv.at[h], pair=me + 2)

    def down_late_copy(h):
        src = half_row(h, 1 - side, 1)
        return remote(src, src, down_late.at[h], late_recv.at[h], pair=me - 2)

    def late_copy():
        src = half_row(row, side, 1)
        return remote(src, src, fwd_send.at[lines], late_recv.at[row], pair=mate)

    def fwd_copy(h):
        src = half_row(h, side, 0)
        return remote(src, src, fwd_send.at[h], fwd_recv.at[h], pair=mate)

    def line_arrived(h):
        remote(own_row(h), own_row(h), up_send.at[0], ag_recv.at[h], pair=mate).wait_recv()

    def late_arrived(h):
        here = half_row(h, 1 - side, 1)
        remote(here, here, up_late.at[0], late_recv.at[h], pair=mate).wait_recv()

    def fwd_arrived(h):
        here = half_row(h, 1 - side, 0)
        remote(here, here, fwd_send.at[0], fwd_recv.at[h], pair=mate).wait_recv()

    def block_copy(d):
        here = blocks_all.at[pl.ds(aux * owned, owned)]
        return remote(here, here, blk_send.at[d], blk_recv.at[aux], aux=(aux + d) % n_aux)

    late_copy().start()

    @pl.when(row + 1 < lines)
    def _():
        up_copy(row).start()

    @pl.when(row > 0)
    def _():
        down_copy(row).start()

    fwd_copy(row).start()
    loop(1, n_aux, lambda d: block_copy(d).start())

    def late_step(h, up, down):
        late_arrived(h)

        @pl.when(up)
        def _():
            up_late_copy(h).start()

        @pl.when(down)
        def _():
            down_late_copy(h).start()

    def line_step(s):
        @pl.when(row - s >= 0)
        def _():
            line_arrived(row - s)

            @pl.when(row + 1 < lines)
            def _():
                up_copy(row - s).start()

            fwd_copy(row - s).start()

        @pl.when(row + s < lines)
        def _():
            line_arrived(row + s)

            @pl.when(row > 0)
            def _():
                down_copy(row + s).start()

            fwd_copy(row + s).start()

        @pl.when(row - s >= 0)
        def _():
            late_step(row - s, row + 1 < lines, row < 0)

        @pl.when(row + s < lines)
        def _():
            late_step(row + s, row < 0, row > 0)

    def clear(h):
        for k in range(3):
            zrecv[k, h] = jnp.zeros(zrecv.shape[2:], BF16)

    @pl.when(row == 0)
    def _():
        loop(0, lines, clear)

    @pl.when(row == lines - 1)
    def _():
        loop(0, lines - 1, clear)
        clear(lines)

    for copy in staged[2:]:
        copy.wait()

    group = 4 if resident % 4 == 0 else 1
    some = range(group)

    def push_pairs(i):
        for p in (2 * i, 2 * i + 1):
            own = amps_all[me * resident + p]
            over = [inter[p * neighbours + k] for k in range(neighbours)]
            half = [mm(x, own, 0, 0).astype(BF16) for x in over]
            for k in range(neighbours):
                push[p * neighbours + k] = mm(half[k], over[k]).astype(BF16)

    loop(0, resident // 2, push_pairs)

    chunk = 16

    def gathered(owner, part_at, emit):
        entry, slot = [], []
        for p in range(resident):
            e, s = p * neighbours, jnp.int32(-1)
            for k in range(neighbours):
                hit = owners[k, p] == owner
                e = jnp.where(hit, p * neighbours + k, e)
                s = jnp.where(hit, slots[k, p], s)
            entry.append(e)
            slot.append(s)
        weight = [
            [jnp.where(slot[p] == part_at * half_slots + j, 1.0, 0.0).astype(F32) for p in range(resident)]
            for j in range(half_slots)
        ]

        def rows(c):
            at = pl.ds(pl.multiple_of(c * chunk, chunk), chunk)
            found = [push[entry[p], at, :].astype(F32) for p in range(resident)]
            for j in range(half_slots):
                total = weight[j][0] * found[0]
                for p in range(1, resident):
                    total = total + weight[j][p] * found[p]
                emit(j, at, total)

        loop(0, width // chunk, rows)

    def x_copy(h):
        return remote(sending.at[h], xrecv.at[h], rx_send.at[h], rx_recv.at[h], pair=mate)

    def x_send(d):
        h = (row + d) % lines

        def emit(j, at, total):
            sending[h, j, at, :] = total.astype(BF16)

        gathered(h * 2 + 1 - side, 0, emit)
        x_copy(h).start()

    def z_copy(k, h, up):
        slot = h if up else jnp.where(h == row - 1, lines, h)
        return remote(
            zsend.at[k, h], zrecv.at[k, slot], rz_send.at[k, h], rz_recv.at[k, slot], pair=me + 2 if up else me - 2
        )

    def z_arrived(k, slot):
        here = zrecv.at[k, slot]
        remote(here, here, rz_send.at[k, 0], rz_recv.at[k, slot], pair=mate).wait_recv()

    def z_send(k, early, h, inner, up):
        @pl.when(inner)
        def _():
            z_arrived(k, h)

        if early:
            x_copy(h).wait_recv()

        def emit(j, at, total):
            total = total + zrecv[k, h, j, at, :].astype(F32)
            if early:
                total = total + xrecv[h, j, at, :].astype(F32)
            zsend[k, h, j, at, :] = total.astype(BF16)

        gathered(h * 2 + side if early else h * 2 + (side + k - 1) % 2, 0 if early else 1, emit)
        z_copy(k, h, up).start()

    def z_step(k, early, s):
        @pl.when(row < s)
        def _():
            z_send(k, early, lines - s + row, row > 0, True)

        @pl.when(lines - 1 - row < s)
        def _():
            z_send(k, early, s - lines + row, row < lines - 1, False)

    def z_last(k):
        @pl.when(row > 0)
        def _():
            z_arrived(k, row)

        @pl.when(row < lines - 1)
        def _():
            z_arrived(k, lines)

    def z_both(k, j, at):
        return zrecv[k, row, j, at, :].astype(F32) + zrecv[k, lines, j, at, :].astype(F32)

    def block_arrived(d):
        src = (aux + d) % n_aux
        here = blocks_all.at[pl.ds(src * owned, owned)]
        remote(here, here, blk_send.at[0], blk_recv.at[src], aux=src).wait_recv()

    def integral(i):
        pairs = [i * group + g for g in some]
        rot = [rotation[p] for p in pairs]
        gram = [mm(blocks_all[domains[0, p]], blocks_all[domains[1, p]], 0, 0).astype(BF16) for p in pairs]
        right = [mm(gram[g], rot[g]).astype(BF16) for g in some]
        for g in some:
            base[pairs[g]] = mm(rot[g], right[g], 0, 0)

    late_step(row, row + 1 < lines, row > 0)
    loop(1, lines + 1, x_send)
    groups = resident // group

    def step(s):
        line_step(s)
        loop(1, 3, lambda k: z_step(k, False, s))

        @pl.when(s == 1)
        def _():
            loop(1, n_aux, block_arrived)

        @pl.when(s <= groups)
        def _():
            integral(s - 1)

    loop(1, lines, step)
    loop(lines - 1, groups, integral)
    loop(1, lines - 1, lambda s: z_step(0, True, s))

    z_last(2)
    last_copy = remote(last_send, last_recv, last_sems.at[0], last_sems.at[1], pair=mate)

    def emit_mate(j, at, total):
        last_send[j, at, :] = (total + z_both(2, j, at)).astype(BF16)

    gathered(mate, 1, emit_mate)
    last_copy.start()
    z_step(0, True, lines - 1)

    loop(0, lines, fwd_arrived)

    def pull_pairs(i):
        for p in (2 * i, 2 * i + 1):
            over = [inter[p * neighbours + k] for k in range(neighbours)]
            half = [
                mm(over[k], amps_all[owners[k, p] * resident + slots[k, p]]).astype(BF16) for k in range(neighbours)
            ]
            total = base[p]
            for k in range(neighbours):
                total = total - mm(half[k], over[k], 1, 1)
            level = jnp.broadcast_to(energies[pl.ds(p, 1), :], (width, width))
            denom = level + level.T
            own = amps_all[me * resident + p].astype(F32)
            inverse = 1.0 / (denom + 1.0)
            rcp[p] = inverse
            base[p] = own - (total + denom * own) * inverse

    loop(0, resident // 2, pull_pairs)

    def own_late(j, at, total):
        total = total + z_both(1, j, at) + last_recv[j, at, :].astype(F32)
        p = half_slots + j
        base[p, at, :] += total * rcp[p, at, :]

    def own_early(j, at, total):
        total = total + z_both(0, j, at) + xrecv[row, j, at, :].astype(F32)
        base[j, at, :] += total * rcp[j, at, :]

    def finish(q):
        pairs = [q * half_slots + g for g in range(half_slots)]
        fresh = [base[p].astype(BF16) for p in pairs]
        for p, x in zip(pairs, fresh):
            new_amps[p] = x
        rot = [rotation[p] for p in pairs]
        pair_density = [(mm(x, x, 1, 1) * (1.0 / width)).astype(BF16) for x in fresh]
        rotated = [mm(r, x).astype(BF16) for r, x in zip(rot, pair_density)]
        for p, r, x in zip(pairs, rot, rotated):
            part[p] = mm(x, r, 1, 1)

    z_last(1)
    last_copy.wait_recv()
    gathered(me, 1, own_late)
    finish(1)
    z_last(0)
    x_copy(row).wait_recv()
    gathered(me, 0, own_early)
    finish(0)

    def t_copy(d):
        t = (me + d) % n
        return remote(part_send.at[t], part_recv.at[me], t_send.at[d], t_recv.at[me], pair=t)

    def tile_part(t, j):
        total = jnp.where(tiles[0] == t * held + j, 1.0, 0.0).astype(F32) * part[0]
        for p in range(1, resident):
            total = total + jnp.where(tiles[p] == t * held + j, 1.0, 0.0).astype(F32) * part[p]
        return total

    def tile_send(d):
        t = (me + d) % n
        for j in range(held):
            part_send[t, j] = tile_part(t, j).astype(BF16)
        t_copy(d).start()

    loop(1, n, tile_send)
    for j in range(held):
        part_own[j] = tile_part(me, j)

    def tile_add(d):
        src = (me + d) % n
        here = part_recv.at[src]
        remote(here, here, t_send.at[0], t_recv.at[src], pair=src).wait_recv()
        for j in range(held):
            part_own[j] += part_recv[src, j].astype(F32)

    loop(1, n, tile_add)
    tot_send[...] = part_own[...].astype(BF16)

    def a_copy(d):
        return remote(tot_send, tot_recv.at[aux], a_send.at[d], a_recv.at[aux], aux=(aux + d) % n_aux)

    loop(1, n_aux, lambda d: a_copy(d).start())

    def tot_add(d):
        src = (aux + d) % n_aux
        here = tot_recv.at[src]
        remote(here, here, a_send.at[0], a_recv.at[src], aux=src).wait_recv()
        for j in range(held):
            part_own[j] += tot_recv[src, j].astype(F32)

    loop(1, n_aux, tot_add)
    for j in range(held):
        total = part_own[j]
        high = total.astype(BF16)
        low = (total - high.astype(F32)).astype(BF16)
        density[j] = (mm(high, coeffs[j]) + mm(low, coeffs[j])) * factor

    def line_left(h):
        @pl.when((row + 1 < lines) & (h <= row))
        def _():
            up_copy(h).wait_send()
            up_late_copy(h).wait_send()

        @pl.when((row > 0) & (h >= row))
        def _():
            down_copy(h).wait_send()
            down_late_copy(h).wait_send()

        fwd_copy(h).wait_send()
        x_copy(h).wait_send()

        @pl.when(h > row)
        def _():
            for k in range(3):
                z_copy(k, h, True).wait_send()

        @pl.when(h < row)
        def _():
            for k in range(3):
                z_copy(k, h, False).wait_send()

    loop(0, lines, line_left)
    late_copy().wait_send()
    last_copy.wait_send()
    loop(1, n_aux, lambda d: block_copy(d).wait_send())
    loop(1, n, lambda d: t_copy(d).wait_send())
    loop(1, n_aux, lambda d: a_copy(d).wait_send())


def local(n, n_aux, amps, rotation, intersections, energies, domains, owners, slots, tiles, blocks, coeffs):
    resident, width = amps.shape[0], amps.shape[1]
    neighbours = owners.shape[1]
    entries = resident * neighbours
    lines = n // 2
    held = coeffs.shape[0]
    square = (width, width)
    dma = pltpu.SemaphoreType.DMA
    scratch = [
        (rotation.shape, BF16),
        ((entries,) + square, BF16),
        (energies.shape, F32),
        (coeffs.shape, BF16),
        ((n * resident,) + square, BF16),
        ((n_aux * blocks.shape[0],) + blocks.shape[1:], BF16),
        ((entries,) + square, BF16),
        ((lines, resident // 2) + square, BF16),
        ((lines, resident // 2) + square, BF16),
        ((3, lines, resident // 2) + square, BF16),
        ((3, lines + 1, resident // 2) + square, BF16),
        ((resident // 2,) + square, BF16),
        ((resident // 2,) + square, BF16),
        ((resident,) + square, F32),
        ((resident,) + square, F32),
        ((resident,) + square, F32),
        ((held,) + square, F32),
        ((n, held) + square, BF16),
        ((n, held) + square, BF16),
        ((held,) + square, BF16),
        ((n_aux, held) + square, BF16),
    ]
    sems = [10] + [lines] * 6 + [lines + 1, lines, n_aux, n_aux, lines, lines, (3, lines), (3, lines + 1), 2]
    sems += [n, n, n_aux, n_aux]
    hbm = pl.BlockSpec(memory_space=pltpu.HBM)
    vmem = pl.BlockSpec(memory_space=pltpu.VMEM)
    out_shape = (
        jax.ShapeDtypeStruct(amps.shape, BF16),
        jax.ShapeDtypeStruct((held, width, coeffs.shape[2]), F32),
    )
    return pl.pallas_call(
        functools.partial(kernel, n, lines, n_aux, neighbours, 1.0 / (resident * n_aux)),
        out_shape=out_shape,
        in_specs=[hbm] * 10,
        out_specs=(vmem, vmem),
        scratch_shapes=[pltpu.SMEM(x.shape, jnp.int32) for x in (owners.T, slots.T, domains.T, tiles)]
        + [pltpu.VMEM(*s) for s in scratch]
        + [dma(k if isinstance(k, tuple) else (k,)) for k in sems],
        compiler_params=pltpu.CompilerParams(
            collective_id=0, has_side_effects=True, vmem_limit_bytes=60 << 20
        ),
    )(
        owners.T,
        slots.T,
        domains.T,
        tiles,
        amps,
        rotation,
        intersections.reshape((entries,) + square),
        energies,
        blocks,
        coeffs,
    )


def solution(mesh):
    return jax.shard_map(
        functools.partial(local, mesh.shape["pair"], mesh.shape["aux"]),
        mesh=mesh,
        in_specs=(
            P(("pair", "aux"), None, None),
            P(("pair", "aux"), None, None),
            P(("pair", "aux"), None, None, None),
            P(("pair", "aux"), None),
            P(("pair", "aux"), None),
            P(("pair", "aux"), None),
            P(("pair", "aux"), None),
            P(("pair", "aux")),
            P("aux", None, None),
            P("pair", None, "aux"),
        ),
        out_specs=(P(("pair", "aux"), None, None), P("pair", None, "aux")),
        check_vma=False,
    )
```

```python
import functools

import jax
import jax.numpy as jnp
from jax import lax
from jax.experimental import pallas as pl
from jax.experimental.pallas import tpu as pltpu
from jax.sharding import PartitionSpec as P

MESH = pl.DeviceIdType.MESH
F32 = jnp.float32
BF16 = jnp.bfloat16


def mm(a, b, ca=1, cb=0):
    return lax.dot_general(a, b, (((ca,), (cb,)), ((), ())), preferred_element_type=F32)


def loop(lo, hi, body):
    def step(i, carry):
        body(i)
        return carry

    lax.fori_loop(lo, hi, step, 0)


def remote(src, dst, send, recv, **where):
    return pltpu.make_async_remote_copy(
        src_ref=src, dst_ref=dst, send_sem=send, recv_sem=recv, device_id=where, device_id_type=MESH
    )


def kernel(
    n, lines, n_aux, neighbours,
    owners_in, slots_in, domains_in, tiles_in,
    amps_in, rotation_in, inter_in, energies_in, blocks_in,
    new_amps, total,
    owners, slots, domains, tiles, rotation, inter, energies,
    amps_all, blocks_all, push, sending, xrecv, zsend, zrecv, last_send, last_recv,
    base, rcp, own_term, part, part_own, part_send, part_recv, tot_send, tot_recv,
    in_sem, up_send, down_send, ag_recv, up_late, down_late, late_recv, fwd_send, fwd_recv, blk_send, blk_recv,
    rx_send, rx_recv, rz_send, rz_recv, last_sems,
    t_send, t_recv, a_send, a_recv,
):
    resident, width = amps_in.shape[0], amps_in.shape[1]
    owned = blocks_in.shape[0]
    held = part_own.shape[0]
    me = lax.axis_index("pair")
    aux = lax.axis_index("aux")
    row, side = me // 2, me % 2
    mate = row * 2 + 1 - side

    def rows_of(src):
        return amps_all.at[pl.ds(src * resident, resident)]

    staged = [
        pltpu.make_async_copy(src, dst, in_sem.at[i])
        for i, (src, dst) in enumerate([
            (amps_in, rows_of(me)),
            (blocks_in, blocks_all.at[pl.ds(aux * owned, owned)]),
            (inter_in, inter),
            (owners_in, owners),
            (slots_in, slots),
            (domains_in, domains),
            (tiles_in, tiles),
            (energies_in, energies),
            (rotation_in, rotation),
        ])
    ]
    for copy in staged:
        copy.start()

    barrier = pltpu.get_barrier_semaphore()

    def greet_pair(d):
        pl.semaphore_signal(barrier, inc=1, device_id={"pair": (me + d) % n}, device_id_type=MESH)

    def greet_aux(d):
        pl.semaphore_signal(barrier, inc=1, device_id={"aux": (aux + d) % n_aux}, device_id_type=MESH)

    loop(1, n, greet_pair)
    loop(1, n_aux, greet_aux)
    staged[0].wait()
    staged[1].wait()
    pl.semaphore_wait(barrier, n - 1 + n_aux - 1)

    half_slots = resident // 2

    def own_row(h):
        return rows_of(h * 2 + side)

    def half_row(h, column, q):
        return amps_all.at[pl.ds((h * 2 + column) * resident + q * half_slots, half_slots)]

    def up_copy(h):
        return remote(own_row(h), own_row(h), up_send.at[h], ag_recv.at[h], pair=me + 2)

    def down_copy(h):
        return remote(own_row(h), own_row(h), down_send.at[h], ag_recv.at[h], pair=me - 2)

    def up_late_copy(h):
        src = half_row(h, 1 - side, 1)
        return remote(src, src, up_late.at[h], late_recv.at[h], pair=me + 2)

    def down_late_copy(h):
        src = half_row(h, 1 - side, 1)
        return remote(src, src, down_late.at[h], late_recv.at[h], pair=me - 2)

    def late_copy():
        src = half_row(row, side, 1)
        return remote(src, src, fwd_send.at[lines], late_recv.at[row], pair=mate)

    def fwd_copy(h):
        src = half_row(h, side, 0)
        return remote(src, src, fwd_send.at[h], fwd_recv.at[h], pair=mate)

    def line_arrived(h):
        remote(own_row(h), own_row(h), up_send.at[0], ag_recv.at[h], pair=mate).wait_recv()

    def late_arrived(h):
        here = half_row(h, 1 - side, 1)
        remote(here, here, up_late.at[0], late_recv.at[h], pair=mate).wait_recv()

    def fwd_arrived(h):
        here = half_row(h, 1 - side, 0)
        remote(here, here, fwd_send.at[0], fwd_recv.at[h], pair=mate).wait_recv()

    def block_copy(d):
        here = blocks_all.at[pl.ds(aux * owned, owned)]
        return remote(here, here, blk_send.at[d], blk_recv.at[aux], aux=(aux + d) % n_aux)

    late_copy().start()

    @pl.when(row + 1 < lines)
    def _():
        up_copy(row).start()

    @pl.when(row > 0)
    def _():
        down_copy(row).start()

    fwd_copy(row).start()
    loop(1, n_aux, lambda d: block_copy(d).start())

    def late_step(h, up, down):
        late_arrived(h)

        @pl.when(up)
        def _():
            up_late_copy(h).start()

        @pl.when(down)
        def _():
            down_late_copy(h).start()

    def line_step(s):
        @pl.when(row - s >= 0)
        def _():
            line_arrived(row - s)

            @pl.when(row + 1 < lines)
            def _():
                up_copy(row - s).start()

            fwd_copy(row - s).start()

        @pl.when(row + s < lines)
        def _():
            line_arrived(row + s)

            @pl.when(row > 0)
            def _():
                down_copy(row + s).start()

            fwd_copy(row + s).start()

        @pl.when(row - s >= 0)
        def _():
            late_step(row - s, row + 1 < lines, row < 0)

        @pl.when(row + s < lines)
        def _():
            late_step(row + s, row < 0, row > 0)

    def clear(h):
        for k in range(3):
            zrecv[k, h] = jnp.zeros(zrecv.shape[2:], BF16)

    @pl.when(row == 0)
    def _():
        loop(0, lines, clear)

    @pl.when(row == lines - 1)
    def _():
        loop(0, lines - 1, clear)
        clear(lines)

    for copy in staged[2:]:
        copy.wait()

    group = 4 if resident % 4 == 0 else 1
    some = range(group)

    def push_pairs(i):
        for p in (2 * i, 2 * i + 1):
            own = amps_all[me * resident + p]
            over = [inter[p * neighbours + k] for k in range(neighbours)]
            half = [mm(x, own, 0, 0).astype(BF16) for x in over]
            for k in range(neighbours):
                push[p * neighbours + k] = mm(half[k], over[k]).astype(BF16)

    loop(0, resident // 2, push_pairs)

    chunk = 16

    def gathered(owner, part_at, emit):
        entry, slot = [], []
        for p in range(resident):
            e, s = p * neighbours, jnp.int32(-1)
            for k in range(neighbours):
                hit = owners[k, p] == owner
                e = jnp.where(hit, p * neighbours + k, e)
                s = jnp.where(hit, slots[k, p], s)
            entry.append(e)
            slot.append(s)
        weight = [
            [jnp.where(slot[p] == part_at * half_slots + j, 1.0, 0.0).astype(F32) for p in range(resident)]
            for j in range(half_slots)
        ]

        def rows(c):
            at = pl.ds(pl.multiple_of(c * chunk, chunk), chunk)
            found = [push[entry[p], at, :].astype(F32) for p in range(resident)]
            for j in range(half_slots):
                total = weight[j][0] * found[0]
                for p in range(1, resident):
                    total = total + weight[j][p] * found[p]
                emit(j, at, total)

        loop(0, width // chunk, rows)

    def x_copy(h):
        return remote(sending.at[h], xrecv.at[h], rx_send.at[h], rx_recv.at[h], pair=mate)

    def x_send(i):
        h = (row + jnp.where(2 * row < lines, 2 * lines - i, i)) % lines

        def emit(j, at, total):
            sending[h, j, at, :] = total.astype(BF16)

        gathered(h * 2 + 1 - side, 0, emit)
        x_copy(h).start()

    def z_copy(k, h, up):
        slot = h if up else jnp.where(h == row - 1, lines, h)
        return remote(
            zsend.at[k, h], zrecv.at[k, slot], rz_send.at[k, h], rz_recv.at[k, slot], pair=me + 2 if up else me - 2
        )

    def z_arrived(k, slot):
        here = zrecv.at[k, slot]
        remote(here, here, rz_send.at[k, 0], rz_recv.at[k, slot], pair=mate).wait_recv()

    def z_send(k, early, h, inner, up):
        @pl.when(inner)
        def _():
            z_arrived(k, h)

        if early:
            x_copy(h).wait_recv()

        def emit(j, at, total):
            total = total + zrecv[k, h, j, at, :].astype(F32)
            if early:
                total = total + xrecv[h, j, at, :].astype(F32)
            zsend[k, h, j, at, :] = total.astype(BF16)

        gathered(h * 2 + side if early else h * 2 + (side + k - 1) % 2, 0 if early else 1, emit)
        z_copy(k, h, up).start()

    def z_step(k, early, s, ends):
        @pl.when((row < s) & ((row == 0) == ends))
        def _():
            z_send(k, early, lines - s + row, row > 0, True)

        @pl.when((lines - 1 - row < s) & ((row == lines - 1) == ends))
        def _():
            z_send(k, early, s - lines + row, row < lines - 1, False)

    def z_last(k):
        @pl.when(row > 0)
        def _():
            z_arrived(k, row)

        @pl.when(row < lines - 1)
        def _():
            z_arrived(k, lines)

    def z_both(k, j, at):
        return zrecv[k, row, j, at, :].astype(F32) + zrecv[k, lines, j, at, :].astype(F32)

    def block_arrived(d):
        src = (aux + d) % n_aux
        here = blocks_all.at[pl.ds(src * owned, owned)]
        remote(here, here, blk_send.at[0], blk_recv.at[src], aux=src).wait_recv()

    def integral(i):
        pairs = [i * group + g for g in some]
        rot = [rotation[p] for p in pairs]
        gram = [mm(blocks_all[domains[0, p]], blocks_all[domains[1, p]], 0, 0).astype(BF16) for p in pairs]
        right = [mm(gram[g], rot[g]).astype(BF16) for g in some]
        for p, r, x in zip(pairs, rot, right):
            base[p] = mm(r, x, 0, 0)
            level = jnp.broadcast_to(energies[pl.ds(p, 1), :], (width, width))
            denom = level + level.T
            own = amps_all[me * resident + p].astype(F32)
            inverse = 1.0 / (denom + 1.0)
            rcp[p] = inverse
            own_term[p] = own - denom * own * inverse

    late_step(row, row + 1 < lines, row > 0)
    x_send(1)
    loop(1, lines, lambda s: loop(1, 3, lambda k: z_step(k, False, s, True)))
    loop(2, lines + 1, x_send)
    groups = resident // group

    def step(s):
        line_step(s)
        loop(1, 3, lambda k: z_step(k, False, s, False))
        z_step(0, True, s, True)

        @pl.when(s == 1)
        def _():
            loop(1, n_aux, block_arrived)

        @pl.when(s <= groups)
        def _():
            integral(s - 1)

    loop(1, lines, step)
    loop(lines - 1, groups, integral)

    z_last(2)
    last_copy = remote(last_send, last_recv, last_sems.at[0], last_sems.at[1], pair=mate)

    def emit_mate(j, at, total):
        last_send[j, at, :] = (total + z_both(2, j, at)).astype(BF16)

    gathered(mate, 1, emit_mate)
    last_copy.start()

    loop(0, lines, fwd_arrived)

    def pull_pairs(i):
        for p in (2 * i, 2 * i + 1):
            over = [inter[p * neighbours + k] for k in range(neighbours)]
            half = [
                mm(over[k], amps_all[owners[k, p] * resident + slots[k, p]]).astype(BF16) for k in range(neighbours)
            ]
            total = base[p]
            for k in range(neighbours):
                total = total - mm(half[k], over[k], 1, 1)
            base[p] = own_term[p] - total * rcp[p]

    def pull_step(s):
        z_step(0, True, s, False)

        @pl.when(s - 2 < resident // 2)
        def _():
            pull_pairs(s - 2)

    loop(2, lines, pull_step)
    loop(lines - 2, resident // 2, pull_pairs)

    def own_late(j, at, total):
        p = half_slots + j
        base[p, at, :] += total * rcp[p, at, :]

    def own_early(j, at, total):
        base[j, at, :] += total * rcp[j, at, :]

    gathered(me, 1, own_late)
    gathered(me, 0, own_early)

    def finish(q, k, other):
        pairs = [q * half_slots + g for g in range(half_slots)]
        fresh = []
        for j, p in enumerate(pairs):
            outside = zrecv[k, row, j].astype(F32) + zrecv[k, lines, j].astype(F32) + other[j].astype(F32)
            fresh.append((base[p] + outside * rcp[p]).astype(BF16))
        for p, x in zip(pairs, fresh):
            new_amps[p] = x
        rot = [rotation[p] for p in pairs]
        pair_density = [(mm(x, x, 1, 1) * (1.0 / width)).astype(BF16) for x in fresh]
        rotated = [mm(r, x).astype(BF16) for r, x in zip(rot, pair_density)]
        for p, r, x in zip(pairs, rot, rotated):
            part[p] = mm(x, r, 1, 1)

    z_last(1)
    last_copy.wait_recv()
    finish(1, 1, last_recv)
    z_last(0)
    x_copy(row).wait_recv()
    finish(0, 0, xrecv.at[row])

    def t_copy(d):
        t = (me + d) % n
        return remote(part_send.at[t], part_recv.at[me], t_send.at[d], t_recv.at[me], pair=t)

    def tile_part(t, j):
        total = jnp.where(tiles[0] == t * held + j, 1.0, 0.0).astype(F32) * part[0]
        for p in range(1, resident):
            total = total + jnp.where(tiles[p] == t * held + j, 1.0, 0.0).astype(F32) * part[p]
        return total

    def tile_send(d):
        t = (me + d) % n
        for j in range(held):
            part_send[t, j] = tile_part(t, j).astype(BF16)
        t_copy(d).start()

    loop(1, n, tile_send)
    for j in range(held):
        part_own[j] = tile_part(me, j)

    def tile_add(d):
        src = (me + d) % n
        here = part_recv.at[src]
        remote(here, here, t_send.at[0], t_recv.at[src], pair=src).wait_recv()
        for j in range(held):
            part_own[j] += part_recv[src, j].astype(F32)

    loop(1, n, tile_add)
    tot_send[...] = part_own[...].astype(BF16)

    def a_copy(d):
        return remote(tot_send, tot_recv.at[aux], a_send.at[d], a_recv.at[aux], aux=(aux + d) % n_aux)

    loop(1, n_aux, lambda d: a_copy(d).start())

    def tot_add(d):
        src = (aux + d) % n_aux
        here = tot_recv.at[src]
        remote(here, here, a_send.at[0], a_recv.at[src], aux=src).wait_recv()
        for j in range(held):
            part_own[j] += tot_recv[src, j].astype(F32)

    loop(1, n_aux, tot_add)
    for j in range(held):
        total[j] = part_own[j]

    def line_left(h):
        @pl.when((row + 1 < lines) & (h <= row))
        def _():
            up_copy(h).wait_send()
            up_late_copy(h).wait_send()

        @pl.when((row > 0) & (h >= row))
        def _():
            down_copy(h).wait_send()
            down_late_copy(h).wait_send()

        fwd_copy(h).wait_send()
        x_copy(h).wait_send()

        @pl.when(h > row)
        def _():
            for k in range(3):
                z_copy(k, h, True).wait_send()

        @pl.when(h < row)
        def _():
            for k in range(3):
                z_copy(k, h, False).wait_send()

    loop(0, lines, line_left)
    late_copy().wait_send()
    last_copy.wait_send()
    loop(1, n_aux, lambda d: block_copy(d).wait_send())
    loop(1, n, lambda d: t_copy(d).wait_send())
    loop(1, n_aux, lambda d: a_copy(d).wait_send())


def finishing(factor, fresh, total_in, coeffs_in, new_amps, density, coeffs, total, result, sems):
    load = pltpu.make_async_copy(coeffs_in, coeffs, sems.at[0])
    load.start()
    sums = pltpu.make_async_copy(total_in, total, sems.at[2])
    sums.start()
    keep = pltpu.make_async_copy(fresh, new_amps, sems.at[1])
    keep.start()
    sums.wait()
    load.wait()
    held = coeffs.shape[0]
    stores = [pltpu.make_async_copy(result.at[j], density.at[j], sems.at[3 + j]) for j in range(held)]
    for j in range(held):
        high = total[j].astype(BF16)
        low = (total[j] - high.astype(F32)).astype(BF16)
        result[j] = (mm(high, coeffs[j]) + mm(low, coeffs[j])) * factor
        stores[j].start()
    for store in stores:
        store.wait()
    keep.wait()


def local(n, n_aux, amps, rotation, intersections, energies, domains, owners, slots, tiles, blocks, coeffs):
    resident, width = amps.shape[0], amps.shape[1]
    neighbours = owners.shape[1]
    entries = resident * neighbours
    lines = n // 2
    held = coeffs.shape[0]
    square = (width, width)
    dma = pltpu.SemaphoreType.DMA
    scratch = [
        (rotation.shape, BF16),
        ((entries,) + square, BF16),
        (energies.shape, F32),
        ((n * resident,) + square, BF16),
        ((n_aux * blocks.shape[0],) + blocks.shape[1:], BF16),
        ((entries,) + square, BF16),
        ((lines, resident // 2) + square, BF16),
        ((lines, resident // 2) + square, BF16),
        ((3, lines, resident // 2) + square, BF16),
        ((3, lines + 1, resident // 2) + square, BF16),
        ((resident // 2,) + square, BF16),
        ((resident // 2,) + square, BF16),
        ((resident,) + square, F32),
        ((resident,) + square, F32),
        ((resident,) + square, F32),
        ((resident,) + square, F32),
        ((held,) + square, F32),
        ((n, held) + square, BF16),
        ((n, held) + square, BF16),
        ((held,) + square, BF16),
        ((n_aux, held) + square, BF16),
    ]
    sems = [9] + [lines] * 6 + [lines + 1, lines, n_aux, n_aux, lines, lines, (3, lines), (3, lines + 1), 2]
    sems += [n, n, n_aux, n_aux]
    hbm = pl.BlockSpec(memory_space=pltpu.HBM)
    vmem = pl.BlockSpec(memory_space=pltpu.VMEM)
    out_shape = (
        jax.ShapeDtypeStruct(amps.shape, BF16),
        jax.ShapeDtypeStruct((held,) + square, F32),
    )
    fresh, total = pl.pallas_call(
        functools.partial(kernel, n, lines, n_aux, neighbours),
        out_shape=out_shape,
        in_specs=[hbm] * 9,
        out_specs=(vmem, vmem),
        scratch_shapes=[pltpu.SMEM(x.shape, jnp.int32) for x in (owners.T, slots.T, domains.T, tiles)]
        + [pltpu.VMEM(*s) for s in scratch]
        + [dma(k if isinstance(k, tuple) else (k,)) for k in sems],
        compiler_params=pltpu.CompilerParams(
            collective_id=0, has_side_effects=True, vmem_limit_bytes=60 << 20
        ),
    )(
        owners.T,
        slots.T,
        domains.T,
        tiles,
        amps,
        rotation,
        intersections.reshape((entries,) + square),
        energies,
        blocks,
    )
    return pl.pallas_call(
        functools.partial(finishing, 1.0 / (resident * n_aux)),
        out_shape=(
            jax.ShapeDtypeStruct(amps.shape, BF16),
            jax.ShapeDtypeStruct((held, width, coeffs.shape[2]), F32),
        ),
        in_specs=[hbm] * 3,
        out_specs=(hbm, hbm),
        scratch_shapes=[
            pltpu.VMEM(coeffs.shape, BF16),
            pltpu.VMEM((held,) + square, F32),
            pltpu.VMEM((held, width, coeffs.shape[2]), F32),
            dma((3 + held,)),
        ],
        compiler_params=pltpu.CompilerParams(vmem_limit_bytes=60 << 20),
    )(fresh, total, coeffs)


def solution(mesh):
    return jax.shard_map(
        functools.partial(local, mesh.shape["pair"], mesh.shape["aux"]),
        mesh=mesh,
        in_specs=(
            P(("pair", "aux"), None, None),
            P(("pair", "aux"), None, None),
            P(("pair", "aux"), None, None, None),
            P(("pair", "aux"), None),
            P(("pair", "aux"), None),
            P(("pair", "aux"), None),
            P(("pair", "aux"), None),
            P(("pair", "aux")),
            P("aux", None, None),
            P("pair", None, "aux"),
        ),
        out_specs=(P(("pair", "aux"), None, None), P("pair", None, "aux")),
        check_vma=False,
    )
```

```python
import functools

import jax
import jax.numpy as jnp
from jax import lax
from jax.experimental import pallas as pl
from jax.experimental.pallas import tpu as pltpu
from jax.sharding import PartitionSpec as P

MESH = pl.DeviceIdType.MESH
F32 = jnp.float32
BF16 = jnp.bfloat16


def mm(a, b, ca=1, cb=0):
    return lax.dot_general(a, b, (((ca,), (cb,)), ((), ())), preferred_element_type=F32)


def loop(lo, hi, body):
    def step(i, carry):
        body(i)
        return carry

    lax.fori_loop(lo, hi, step, 0)


def remote(src, dst, send, recv, **where):
    return pltpu.make_async_remote_copy(
        src_ref=src, dst_ref=dst, send_sem=send, recv_sem=recv, device_id=where, device_id_type=MESH
    )


def kernel(
    n, lines, n_aux, neighbours,
    owners_in, slots_in, domains_in, tiles_in,
    amps_in, rotation_in, inter_in, energies_in, blocks_in,
    new_amps, total,
    owners, slots, domains, tiles, rotation, inter, energies,
    amps_all, blocks_all, push, sending, xrecv, zsend, zrecv, last_send, last_recv,
    base, rcp, own_term, part, part_own, part_send, part_recv, tot_send, tot_recv,
    in_sem, up_send, down_send, ag_recv, up_late, down_late, late_recv, fwd_send, fwd_recv, blk_send, blk_recv,
    rx_send, rx_recv, rz_send, rz_recv, last_sems,
    t_send, t_recv, a_send, a_recv,
):
    resident, width = amps_in.shape[0], amps_in.shape[1]
    owned = blocks_in.shape[0]
    held = part_own.shape[0]
    me = lax.axis_index("pair")
    aux = lax.axis_index("aux")
    row, side = me // 2, me % 2
    mate = row * 2 + 1 - side

    def rows_of(src):
        return amps_all.at[pl.ds(src * resident, resident)]

    staged = [
        pltpu.make_async_copy(src, dst, in_sem.at[i])
        for i, (src, dst) in enumerate([
            (amps_in, rows_of(me)),
            (blocks_in, blocks_all.at[pl.ds(aux * owned, owned)]),
            (inter_in, inter),
            (owners_in, owners),
            (slots_in, slots),
            (domains_in, domains),
            (tiles_in, tiles),
            (energies_in, energies),
            (rotation_in, rotation),
        ])
    ]
    for copy in staged:
        copy.start()

    barrier = pltpu.get_barrier_semaphore()

    def greet_pair(d):
        pl.semaphore_signal(barrier, inc=1, device_id={"pair": (me + d) % n}, device_id_type=MESH)

    def greet_aux(d):
        pl.semaphore_signal(barrier, inc=1, device_id={"aux": (aux + d) % n_aux}, device_id_type=MESH)

    loop(1, n, greet_pair)
    loop(1, n_aux, greet_aux)
    staged[0].wait()
    staged[1].wait()
    pl.semaphore_wait(barrier, n - 1 + n_aux - 1)

    half_slots = resident // 2

    def own_row(h):
        return rows_of(h * 2 + side)

    def half_row(h, column, q):
        return amps_all.at[pl.ds((h * 2 + column) * resident + q * half_slots, half_slots)]

    def up_copy(h):
        return remote(own_row(h), own_row(h), up_send.at[h], ag_recv.at[h], pair=me + 2)

    def down_copy(h):
        return remote(own_row(h), own_row(h), down_send.at[h], ag_recv.at[h], pair=me - 2)

    def up_late_copy(h):
        src = half_row(h, 1 - side, 1)
        return remote(src, src, up_late.at[h], late_recv.at[h], pair=me + 2)

    def down_late_copy(h):
        src = half_row(h, 1 - side, 1)
        return remote(src, src, down_late.at[h], late_recv.at[h], pair=me - 2)

    def late_copy():
        src = half_row(row, side, 1)
        return remote(src, src, fwd_send.at[lines], late_recv.at[row], pair=mate)

    def fwd_copy(h):
        src = half_row(h, side, 0)
        return remote(src, src, fwd_send.at[h], fwd_recv.at[h], pair=mate)

    def line_arrived(h):
        remote(own_row(h), own_row(h), up_send.at[0], ag_recv.at[h], pair=mate).wait_recv()

    def late_arrived(h):
        here = half_row(h, 1 - side, 1)
        remote(here, here, up_late.at[0], late_recv.at[h], pair=mate).wait_recv()

    def fwd_arrived(h):
        here = half_row(h, 1 - side, 0)
        remote(here, here, fwd_send.at[0], fwd_recv.at[h], pair=mate).wait_recv()

    def block_copy(d):
        here = blocks_all.at[pl.ds(aux * owned, owned)]
        return remote(here, here, blk_send.at[d], blk_recv.at[aux], aux=(aux + d) % n_aux)

    late_copy().start()

    @pl.when(row + 1 < lines)
    def _():
        up_copy(row).start()

    @pl.when(row > 0)
    def _():
        down_copy(row).start()

    fwd_copy(row).start()
    loop(1, n_aux, lambda d: block_copy(d).start())

    def late_step(h, up, down):
        late_arrived(h)

        @pl.when(up)
        def _():
            up_late_copy(h).start()

        @pl.when(down)
        def _():
            down_late_copy(h).start()

    def line_step(s):
        @pl.when(row - s >= 0)
        def _():
            line_arrived(row - s)

            @pl.when(row + 1 < lines)
            def _():
                up_copy(row - s).start()

            fwd_copy(row - s).start()

        @pl.when(row + s < lines)
        def _():
            line_arrived(row + s)

            @pl.when(row > 0)
            def _():
                down_copy(row + s).start()

            fwd_copy(row + s).start()

        @pl.when(row - s >= 0)
        def _():
            late_step(row - s, row + 1 < lines, row < 0)

        @pl.when(row + s < lines)
        def _():
            late_step(row + s, row < 0, row > 0)

    def clear(h):
        for k in range(3):
            zrecv[k, h] = jnp.zeros(zrecv.shape[2:], BF16)

    @pl.when(row == 0)
    def _():
        loop(0, lines, clear)

    @pl.when(row == lines - 1)
    def _():
        loop(0, lines - 1, clear)
        clear(lines)

    for copy in staged[2:]:
        copy.wait()

    group = 4 if resident % 4 == 0 else 1
    some = range(group)

    def push_pairs(i):
        for p in (2 * i, 2 * i + 1):
            own = amps_all[me * resident + p]
            over = [inter[p * neighbours + k] for k in range(neighbours)]
            half = [mm(x, own, 0, 0).astype(BF16) for x in over]
            for k in range(neighbours):
                push[p * neighbours + k] = mm(half[k], over[k]).astype(BF16)

    loop(0, resident // 2, push_pairs)

    chunk = 16

    def gathered(owner, part_at, emit):
        entry, slot = [], []
        for p in range(resident):
            e, s = p * neighbours, jnp.int32(-1)
            for k in range(neighbours):
                hit = owners[k, p] == owner
                e = jnp.where(hit, p * neighbours + k, e)
                s = jnp.where(hit, slots[k, p], s)
            entry.append(e)
            slot.append(s)
        weight = [
            [jnp.where(slot[p] == part_at * half_slots + j, 1.0, 0.0).astype(F32) for p in range(resident)]
            for j in range(half_slots)
        ]

        def rows(c):
            at = pl.ds(pl.multiple_of(c * chunk, chunk), chunk)
            found = [push[entry[p], at, :].astype(F32) for p in range(resident)]
            for j in range(half_slots):
                total = weight[j][0] * found[0]
                for p in range(1, resident):
                    total = total + weight[j][p] * found[p]
                emit(j, at, total)

        loop(0, width // chunk, rows)

    def x_copy(h):
        return remote(sending.at[h], xrecv.at[h], rx_send.at[h], rx_recv.at[h], pair=mate)

    def x_send(i):
        h = (row + jnp.where(2 * row < lines, 2 * lines - i, i)) % lines

        def emit(j, at, total):
            sending[h, j, at, :] = total.astype(BF16)

        gathered(h * 2 + 1 - side, 0, emit)
        x_copy(h).start()

    def z_copy(k, h, up):
        slot = h if up else jnp.where(h == row - 1, lines, h)
        return remote(
            zsend.at[k, h], zrecv.at[k, slot], rz_send.at[k, h], rz_recv.at[k, slot], pair=me + 2 if up else me - 2
        )

    def z_arrived(k, slot):
        here = zrecv.at[k, slot]
        remote(here, here, rz_send.at[k, 0], rz_recv.at[k, slot], pair=mate).wait_recv()

    def z_send(k, early, h, inner, up):
        @pl.when(inner)
        def _():
            z_arrived(k, h)

        if early:
            x_copy(h).wait_recv()

        def emit(j, at, total):
            total = total + zrecv[k, h, j, at, :].astype(F32)
            if early:
                total = total + xrecv[h, j, at, :].astype(F32)
            zsend[k, h, j, at, :] = total.astype(BF16)

        gathered(h * 2 + side if early else h * 2 + (side + k - 1) % 2, 0 if early else 1, emit)
        z_copy(k, h, up).start()

    def z_step(k, early, s, ends):
        @pl.when((row < s) & ((row == 0) == ends))
        def _():
            z_send(k, early, lines - s + row, row > 0, True)

        @pl.when((lines - 1 - row < s) & ((row == lines - 1) == ends))
        def _():
            z_send(k, early, s - lines + row, row < lines - 1, False)

    def z_last(k):
        @pl.when(row > 0)
        def _():
            z_arrived(k, row)

        @pl.when(row < lines - 1)
        def _():
            z_arrived(k, lines)

    def z_both(k, j, at):
        return zrecv[k, row, j, at, :].astype(F32) + zrecv[k, lines, j, at, :].astype(F32)

    def block_arrived(d):
        src = (aux + d) % n_aux
        here = blocks_all.at[pl.ds(src * owned, owned)]
        remote(here, here, blk_send.at[0], blk_recv.at[src], aux=src).wait_recv()

    def integral(i):
        pairs = [i * group + g for g in some]
        rot = [rotation[p] for p in pairs]
        gram = [mm(blocks_all[domains[0, p]], blocks_all[domains[1, p]], 0, 0).astype(BF16) for p in pairs]
        right = [mm(gram[g], rot[g]).astype(BF16) for g in some]
        for p, r, x in zip(pairs, rot, right):
            base[p] = mm(r, x, 0, 0)
            level = jnp.broadcast_to(energies[pl.ds(p, 1), :], (width, width))
            denom = level + level.T
            own = amps_all[me * resident + p].astype(F32)
            inverse = 1.0 / (denom + 1.0)
            rcp[p] = inverse
            own_term[p] = own - denom * own * inverse

    late_step(row, row + 1 < lines, row > 0)
    x_send(1)
    loop(1, lines, lambda s: loop(1, 3, lambda k: z_step(k, False, s, True)))
    loop(2, lines + 1, x_send)
    groups = resident // group

    def step(s):
        line_step(s)
        loop(1, 3, lambda k: z_step(k, False, s, False))
        z_step(0, True, s, True)

        @pl.when(s == 1)
        def _():
            loop(1, n_aux, block_arrived)

        @pl.when(s <= groups)
        def _():
            integral(s - 1)

    loop(1, lines, step)
    loop(lines - 1, groups, integral)

    z_last(2)
    last_copy = remote(last_send, last_recv, last_sems.at[0], last_sems.at[1], pair=mate)

    def emit_mate(j, at, total):
        last_send[j, at, :] = (total + z_both(2, j, at)).astype(BF16)

    gathered(mate, 1, emit_mate)
    last_copy.start()

    loop(0, lines, fwd_arrived)

    def pull_pairs(i):
        for p in (2 * i, 2 * i + 1):
            over = [inter[p * neighbours + k] for k in range(neighbours)]
            half = [
                mm(over[k], amps_all[owners[k, p] * resident + slots[k, p]]).astype(BF16) for k in range(neighbours)
            ]
            total = base[p]
            for k in range(neighbours):
                total = total - mm(half[k], over[k], 1, 1)
            base[p] = own_term[p] - total * rcp[p]

    def pull_step(s):
        z_step(0, True, s, False)

        @pl.when(s - 2 < resident // 2)
        def _():
            pull_pairs(s - 2)

    loop(2, lines, pull_step)
    loop(lines - 2, resident // 2, pull_pairs)

    def own_late(j, at, total):
        p = half_slots + j
        base[p, at, :] += total * rcp[p, at, :]

    def own_early(j, at, total):
        base[j, at, :] += total * rcp[j, at, :]

    gathered(me, 1, own_late)
    gathered(me, 0, own_early)

    def finish(q, k, other):
        pairs = [q * half_slots + g for g in range(half_slots)]
        fresh = []
        for j, p in enumerate(pairs):
            outside = zrecv[k, row, j].astype(F32) + zrecv[k, lines, j].astype(F32) + other[j].astype(F32)
            fresh.append((base[p] + outside * rcp[p]).astype(BF16))
        for p, x in zip(pairs, fresh):
            new_amps[p] = x
        rot = [rotation[p] for p in pairs]
        pair_density = [(mm(x, x, 1, 1) * (1.0 / width)).astype(BF16) for x in fresh]
        rotated = [mm(r, x).astype(BF16) for r, x in zip(rot, pair_density)]
        for p, r, x in zip(pairs, rot, rotated):
            part[p] = mm(x, r, 1, 1)

    z_last(1)
    last_copy.wait_recv()
    finish(1, 1, last_recv)
    z_last(0)
    x_copy(row).wait_recv()
    finish(0, 0, xrecv.at[row])

    def t_copy(d):
        t = (me + d) % n
        return remote(part_send.at[t], part_recv.at[me], t_send.at[d], t_recv.at[me], pair=t)

    def tile_part(t, j):
        total = jnp.where(tiles[0] == t * held + j, 1.0, 0.0).astype(F32) * part[0]
        for p in range(1, resident):
            total = total + jnp.where(tiles[p] == t * held + j, 1.0, 0.0).astype(F32) * part[p]
        return total

    def tile_send(d):
        t = (me + d) % n
        for j in range(held):
            part_send[t, j] = tile_part(t, j).astype(BF16)
        t_copy(d).start()

    loop(1, n, tile_send)
    for j in range(held):
        part_own[j] = tile_part(me, j)

    def tile_add(d):
        src = (me + d) % n
        here = part_recv.at[src]
        remote(here, here, t_send.at[0], t_recv.at[src], pair=src).wait_recv()
        for j in range(held):
            part_own[j] += part_recv[src, j].astype(F32)

    loop(1, n, tile_add)
    tot_send[...] = part_own[...].astype(BF16)

    def a_copy(d):
        return remote(tot_send, tot_recv.at[aux], a_send.at[d], a_recv.at[aux], aux=(aux + d) % n_aux)

    loop(1, n_aux, lambda d: a_copy(d).start())

    def tot_add(d):
        src = (aux + d) % n_aux
        here = tot_recv.at[src]
        remote(here, here, a_send.at[0], a_recv.at[src], aux=src).wait_recv()
        for j in range(held):
            part_own[j] += tot_recv[src, j].astype(F32)

    loop(1, n_aux, tot_add)
    for j in range(held):
        total[j] = part_own[j]

    def line_left(h):
        @pl.when((row + 1 < lines) & (h <= row))
        def _():
            up_copy(h).wait_send()
            up_late_copy(h).wait_send()

        @pl.when((row > 0) & (h >= row))
        def _():
            down_copy(h).wait_send()
            down_late_copy(h).wait_send()

        fwd_copy(h).wait_send()
        x_copy(h).wait_send()

        @pl.when(h > row)
        def _():
            for k in range(3):
                z_copy(k, h, True).wait_send()

        @pl.when(h < row)
        def _():
            for k in range(3):
                z_copy(k, h, False).wait_send()

    loop(0, lines, line_left)
    late_copy().wait_send()
    last_copy.wait_send()
    loop(1, n_aux, lambda d: block_copy(d).wait_send())
    loop(1, n, lambda d: t_copy(d).wait_send())
    loop(1, n_aux, lambda d: a_copy(d).wait_send())


def finishing(factor, fresh, total_in, coeffs_in, new_amps, density, coeffs, total, result, passing, sems):
    load = pltpu.make_async_copy(coeffs_in, coeffs, sems.at[0])
    load.start()
    sums = pltpu.make_async_copy(total_in, total, sems.at[2])
    sums.start()
    fetch = pltpu.make_async_copy(fresh, passing, sems.at[1])
    fetch.start()
    fetch.wait()
    keep = pltpu.make_async_copy(passing, new_amps, sems.at[3])
    keep.start()
    sums.wait()
    load.wait()
    held = coeffs.shape[0]
    stores = [pltpu.make_async_copy(result.at[j], density.at[j], sems.at[4 + j]) for j in range(held)]
    for j in range(held):
        high = total[j].astype(BF16)
        low = (total[j] - high.astype(F32)).astype(BF16)
        result[j] = (mm(high, coeffs[j]) + mm(low, coeffs[j])) * factor
        stores[j].start()
    for store in stores:
        store.wait()
    keep.wait()


def local(n, n_aux, amps, rotation, intersections, energies, domains, owners, slots, tiles, blocks, coeffs):
    resident, width = amps.shape[0], amps.shape[1]
    neighbours = owners.shape[1]
    entries = resident * neighbours
    lines = n // 2
    held = coeffs.shape[0]
    square = (width, width)
    dma = pltpu.SemaphoreType.DMA
    scratch = [
        (rotation.shape, BF16),
        ((entries,) + square, BF16),
        (energies.shape, F32),
        ((n * resident,) + square, BF16),
        ((n_aux * blocks.shape[0],) + blocks.shape[1:], BF16),
        ((entries,) + square, BF16),
        ((lines, resident // 2) + square, BF16),
        ((lines, resident // 2) + square, BF16),
        ((3, lines, resident // 2) + square, BF16),
        ((3, lines + 1, resident // 2) + square, BF16),
        ((resident // 2,) + square, BF16),
        ((resident // 2,) + square, BF16),
        ((resident,) + square, F32),
        ((resident,) + square, F32),
        ((resident,) + square, F32),
        ((resident,) + square, F32),
        ((held,) + square, F32),
        ((n, held) + square, BF16),
        ((n, held) + square, BF16),
        ((held,) + square, BF16),
        ((n_aux, held) + square, BF16),
    ]
    sems = [9] + [lines] * 6 + [lines + 1, lines, n_aux, n_aux, lines, lines, (3, lines), (3, lines + 1), 2]
    sems += [n, n, n_aux, n_aux]
    hbm = pl.BlockSpec(memory_space=pltpu.HBM)
    vmem = pl.BlockSpec(memory_space=pltpu.VMEM)
    out_shape = (
        jax.ShapeDtypeStruct(amps.shape, BF16),
        jax.ShapeDtypeStruct((held,) + square, F32),
    )
    fresh, total = pl.pallas_call(
        functools.partial(kernel, n, lines, n_aux, neighbours),
        out_shape=out_shape,
        in_specs=[hbm] * 9,
        out_specs=(vmem, vmem),
        scratch_shapes=[pltpu.SMEM(x.shape, jnp.int32) for x in (owners.T, slots.T, domains.T, tiles)]
        + [pltpu.VMEM(*s) for s in scratch]
        + [dma(k if isinstance(k, tuple) else (k,)) for k in sems],
        compiler_params=pltpu.CompilerParams(
            collective_id=0, has_side_effects=True, vmem_limit_bytes=60 << 20
        ),
    )(
        owners.T,
        slots.T,
        domains.T,
        tiles,
        amps,
        rotation,
        intersections.reshape((entries,) + square),
        energies,
        blocks,
    )
    return pl.pallas_call(
        functools.partial(finishing, 1.0 / (resident * n_aux)),
        out_shape=(
            jax.ShapeDtypeStruct(amps.shape, BF16),
            jax.ShapeDtypeStruct((held, width, coeffs.shape[2]), F32),
        ),
        in_specs=[hbm] * 3,
        out_specs=(hbm, hbm),
        scratch_shapes=[
            pltpu.VMEM(coeffs.shape, BF16),
            pltpu.VMEM((held,) + square, F32),
            pltpu.VMEM((held, width, coeffs.shape[2]), F32),
            pltpu.VMEM(amps.shape, BF16),
            dma((4 + held,)),
        ],
        compiler_params=pltpu.CompilerParams(vmem_limit_bytes=60 << 20),
    )(fresh, total, coeffs)


def solution(mesh):
    return jax.shard_map(
        functools.partial(local, mesh.shape["pair"], mesh.shape["aux"]),
        mesh=mesh,
        in_specs=(
            P(("pair", "aux"), None, None),
            P(("pair", "aux"), None, None),
            P(("pair", "aux"), None, None, None),
            P(("pair", "aux"), None),
            P(("pair", "aux"), None),
            P(("pair", "aux"), None),
            P(("pair", "aux"), None),
            P(("pair", "aux")),
            P("aux", None, None),
            P("pair", None, "aux"),
        ),
        out_specs=(P(("pair", "aux"), None, None), P("pair", None, "aux")),
        check_vma=False,
    )
```

```python
import functools

import jax
import jax.numpy as jnp
from jax import lax
from jax.experimental import pallas as pl
from jax.experimental.pallas import tpu as pltpu
from jax.sharding import PartitionSpec as P

MESH = pl.DeviceIdType.MESH
F32 = jnp.float32
BF16 = jnp.bfloat16


def mm(a, b, ca=1, cb=0):
    return lax.dot_general(a, b, (((ca,), (cb,)), ((), ())), preferred_element_type=F32)


def loop(lo, hi, body):
    def step(i, carry):
        body(i)
        return carry

    lax.fori_loop(lo, hi, step, 0)


def remote(src, dst, send, recv, **where):
    return pltpu.make_async_remote_copy(
        src_ref=src, dst_ref=dst, send_sem=send, recv_sem=recv, device_id=where, device_id_type=MESH
    )


def kernel(
    n, lines, n_aux, neighbours,
    owners_in, slots_in, domains_in, tiles_in,
    amps_in, rotation_in, inter_in, energies_in, blocks_in,
    new_amps, total,
    owners, slots, domains, tiles, rotation, inter, energies,
    amps_all, blocks_all, push, sending, xrecv, zsend, zrecv, last_send, last_recv,
    base, rcp, own_term, part, part_own, part_send, part_recv, tot_send, tot_recv,
    in_sem, up_send, down_send, ag_recv, up_late, down_late, late_recv, fwd_send, fwd_recv, blk_send, blk_recv,
    rx_send, rx_recv, rz_send, rz_recv, last_sems,
    t_send, t_recv, a_send, a_recv,
):
    resident, width = amps_in.shape[0], amps_in.shape[1]
    owned = blocks_in.shape[0]
    held = part_own.shape[0]
    me = lax.axis_index("pair")
    aux = lax.axis_index("aux")
    row, side = me // 2, me % 2
    mate = row * 2 + 1 - side

    def rows_of(src):
        return amps_all.at[pl.ds(src * resident, resident)]

    staged = [
        pltpu.make_async_copy(src, dst, in_sem.at[i])
        for i, (src, dst) in enumerate([
            (amps_in, rows_of(me)),
            (blocks_in, blocks_all.at[pl.ds(aux * owned, owned)]),
            (inter_in, inter),
            (owners_in, owners),
            (slots_in, slots),
            (domains_in, domains),
            (tiles_in, tiles),
            (energies_in, energies),
            (rotation_in, rotation),
        ])
    ]
    for copy in staged:
        copy.start()

    barrier = pltpu.get_barrier_semaphore()

    def greet_pair(d):
        pl.semaphore_signal(barrier, inc=1, device_id={"pair": (me + d) % n}, device_id_type=MESH)

    def greet_aux(d):
        pl.semaphore_signal(barrier, inc=1, device_id={"aux": (aux + d) % n_aux}, device_id_type=MESH)

    loop(1, n, greet_pair)
    loop(1, n_aux, greet_aux)
    staged[0].wait()
    staged[1].wait()
    pl.semaphore_wait(barrier, n - 1 + n_aux - 1)

    half_slots = resident // 2

    def own_row(h):
        return rows_of(h * 2 + side)

    def half_row(h, column, q):
        return amps_all.at[pl.ds((h * 2 + column) * resident + q * half_slots, half_slots)]

    def up_copy(h):
        return remote(own_row(h), own_row(h), up_send.at[h], ag_recv.at[h], pair=me + 2)

    def down_copy(h):
        return remote(own_row(h), own_row(h), down_send.at[h], ag_recv.at[h], pair=me - 2)

    def up_late_copy(h):
        src = half_row(h, 1 - side, 1)
        return remote(src, src, up_late.at[h], late_recv.at[h], pair=me + 2)

    def down_late_copy(h):
        src = half_row(h, 1 - side, 1)
        return remote(src, src, down_late.at[h], late_recv.at[h], pair=me - 2)

    def late_copy():
        src = half_row(row, side, 1)
        return remote(src, src, fwd_send.at[lines], late_recv.at[row], pair=mate)

    def fwd_copy(h):
        src = half_row(h, side, 0)
        return remote(src, src, fwd_send.at[h], fwd_recv.at[h], pair=mate)

    def line_arrived(h):
        remote(own_row(h), own_row(h), up_send.at[0], ag_recv.at[h], pair=mate).wait_recv()

    def late_arrived(h):
        here = half_row(h, 1 - side, 1)
        remote(here, here, up_late.at[0], late_recv.at[h], pair=mate).wait_recv()

    def fwd_arrived(h):
        here = half_row(h, 1 - side, 0)
        remote(here, here, fwd_send.at[0], fwd_recv.at[h], pair=mate).wait_recv()

    def block_copy(d):
        here = blocks_all.at[pl.ds(aux * owned, owned)]
        return remote(here, here, blk_send.at[d], blk_recv.at[aux], aux=(aux + d) % n_aux)

    late_copy().start()

    @pl.when(row + 1 < lines)
    def _():
        up_copy(row).start()

    @pl.when(row > 0)
    def _():
        down_copy(row).start()

    fwd_copy(row).start()
    loop(1, n_aux, lambda d: block_copy(d).start())

    def late_step(h, up, down):
        late_arrived(h)

        @pl.when(up)
        def _():
            up_late_copy(h).start()

        @pl.when(down)
        def _():
            down_late_copy(h).start()

    def line_step(s):
        @pl.when(row - s >= 0)
        def _():
            line_arrived(row - s)

            @pl.when(row + 1 < lines)
            def _():
                up_copy(row - s).start()

            fwd_copy(row - s).start()

        @pl.when(row + s < lines)
        def _():
            line_arrived(row + s)

            @pl.when(row > 0)
            def _():
                down_copy(row + s).start()

            fwd_copy(row + s).start()

        @pl.when(row - s >= 0)
        def _():
            late_step(row - s, row + 1 < lines, row < 0)

        @pl.when(row + s < lines)
        def _():
            late_step(row + s, row < 0, row > 0)

    def clear(h):
        for k in range(3):
            zrecv[k, h] = jnp.zeros(zrecv.shape[2:], BF16)

    @pl.when(row == 0)
    def _():
        loop(0, lines, clear)

    @pl.when(row == lines - 1)
    def _():
        loop(0, lines - 1, clear)
        clear(lines)

    for copy in staged[2:]:
        copy.wait()

    group = 4 if resident % 4 == 0 else 1
    some = range(group)

    def push_pairs(i):
        for p in (2 * i, 2 * i + 1):
            own = amps_all[me * resident + p]
            over = [inter[p * neighbours + k] for k in range(neighbours)]
            half = [mm(x, own, 0, 0).astype(BF16) for x in over]
            for k in range(neighbours):
                push[p * neighbours + k] = mm(half[k], over[k]).astype(BF16)

    loop(0, resident // 4, push_pairs)
    late_step(row, row + 1 < lines, row > 0)
    loop(resident // 4, resident // 2, push_pairs)

    chunk = 16

    def gathered(owner, part_at, emit):
        entry, slot = [], []
        for p in range(resident):
            e, s = p * neighbours, jnp.int32(-1)
            for k in range(neighbours):
                hit = owners[k, p] == owner
                e = jnp.where(hit, p * neighbours + k, e)
                s = jnp.where(hit, slots[k, p], s)
            entry.append(e)
            slot.append(s)
        weight = [
            [jnp.where(slot[p] == part_at * half_slots + j, 1.0, 0.0).astype(F32) for p in range(resident)]
            for j in range(half_slots)
        ]

        def rows(c):
            at = pl.ds(pl.multiple_of(c * chunk, chunk), chunk)
            found = [push[entry[p], at, :].astype(F32) for p in range(resident)]
            for j in range(half_slots):
                total = weight[j][0] * found[0]
                for p in range(1, resident):
                    total = total + weight[j][p] * found[p]
                emit(j, at, total)

        loop(0, width // chunk, rows)

    def x_copy(h):
        return remote(sending.at[h], xrecv.at[h], rx_send.at[h], rx_recv.at[h], pair=mate)

    def x_send(i):
        h = (row + jnp.where(2 * row < lines, 2 * lines - i, i)) % lines

        def emit(j, at, total):
            sending[h, j, at, :] = total.astype(BF16)

        gathered(h * 2 + 1 - side, 0, emit)
        x_copy(h).start()

    def z_copy(k, h, up):
        slot = h if up else jnp.where(h == row - 1, lines, h)
        return remote(
            zsend.at[k, h], zrecv.at[k, slot], rz_send.at[k, h], rz_recv.at[k, slot], pair=me + 2 if up else me - 2
        )

    def z_arrived(k, slot):
        here = zrecv.at[k, slot]
        remote(here, here, rz_send.at[k, 0], rz_recv.at[k, slot], pair=mate).wait_recv()

    def z_send(k, early, h, inner, up):
        @pl.when(inner)
        def _():
            z_arrived(k, h)

        if early:
            x_copy(h).wait_recv()

        def emit(j, at, total):
            total = total + zrecv[k, h, j, at, :].astype(F32)
            if early:
                total = total + xrecv[h, j, at, :].astype(F32)
            zsend[k, h, j, at, :] = total.astype(BF16)

        gathered(h * 2 + side if early else h * 2 + (side + k - 1) % 2, 0 if early else 1, emit)
        z_copy(k, h, up).start()

    def z_step(k, early, s, ends):
        @pl.when((row < s) & ((row == 0) == ends))
        def _():
            z_send(k, early, lines - s + row, row > 0, True)

        @pl.when((lines - 1 - row < s) & ((row == lines - 1) == ends))
        def _():
            z_send(k, early, s - lines + row, row < lines - 1, False)

    def z_last(k):
        @pl.when(row > 0)
        def _():
            z_arrived(k, row)

        @pl.when(row < lines - 1)
        def _():
            z_arrived(k, lines)

    def z_both(k, j, at):
        return zrecv[k, row, j, at, :].astype(F32) + zrecv[k, lines, j, at, :].astype(F32)

    def block_arrived(d):
        src = (aux + d) % n_aux
        here = blocks_all.at[pl.ds(src * owned, owned)]
        remote(here, here, blk_send.at[0], blk_recv.at[src], aux=src).wait_recv()

    def integral(i):
        pairs = [i * group + g for g in some]
        rot = [rotation[p] for p in pairs]
        gram = [mm(blocks_all[domains[0, p]], blocks_all[domains[1, p]], 0, 0).astype(BF16) for p in pairs]
        right = [mm(gram[g], rot[g]).astype(BF16) for g in some]
        for p, r, x in zip(pairs, rot, right):
            base[p] = mm(r, x, 0, 0)
            level = jnp.broadcast_to(energies[pl.ds(p, 1), :], (width, width))
            denom = level + level.T
            own = amps_all[me * resident + p].astype(F32)
            inverse = 1.0 / (denom + 1.0)
            rcp[p] = inverse
            own_term[p] = own - denom * own * inverse

    x_send(1)
    loop(1, lines, lambda s: loop(1, 3, lambda k: z_step(k, False, s, True)))
    loop(2, lines + 1, x_send)
    groups = resident // group

    def step(s):
        line_step(s)
        loop(1, 3, lambda k: z_step(k, False, s, False))
        z_step(0, True, s, True)

        @pl.when(s == 1)
        def _():
            loop(1, n_aux, block_arrived)

        @pl.when(s <= groups)
        def _():
            integral(s - 1)

    loop(1, lines, step)
    loop(lines - 1, groups, integral)

    z_last(2)
    last_copy = remote(last_send, last_recv, last_sems.at[0], last_sems.at[1], pair=mate)

    def emit_mate(j, at, total):
        last_send[j, at, :] = (total + z_both(2, j, at)).astype(BF16)

    gathered(mate, 1, emit_mate)
    last_copy.start()

    loop(0, lines, fwd_arrived)

    def pull_pairs(i):
        for p in (2 * i, 2 * i + 1):
            over = [inter[p * neighbours + k] for k in range(neighbours)]
            half = [
                mm(over[k], amps_all[owners[k, p] * resident + slots[k, p]]).astype(BF16) for k in range(neighbours)
            ]
            total = base[p]
            for k in range(neighbours):
                total = total - mm(half[k], over[k], 1, 1)
            base[p] = own_term[p] - total * rcp[p]

    def pull_step(s):
        z_step(0, True, s, False)

        @pl.when(s - 2 < resident // 2)
        def _():
            pull_pairs(s - 2)

    loop(2, lines, pull_step)
    loop(lines - 2, resident // 2, pull_pairs)

    def own_late(j, at, total):
        p = half_slots + j
        base[p, at, :] += total * rcp[p, at, :]

    def own_early(j, at, total):
        base[j, at, :] += total * rcp[j, at, :]

    gathered(me, 1, own_late)
    gathered(me, 0, own_early)

    def finish(q, k, other):
        pairs = [q * half_slots + g for g in range(half_slots)]
        fresh = []
        for j, p in enumerate(pairs):
            outside = zrecv[k, row, j].astype(F32) + zrecv[k, lines, j].astype(F32) + other[j].astype(F32)
            fresh.append((base[p] + outside * rcp[p]).astype(BF16))
        for p, x in zip(pairs, fresh):
            new_amps[p] = x
        rot = [rotation[p] for p in pairs]
        pair_density = [(mm(x, x, 1, 1) * (1.0 / width)).astype(BF16) for x in fresh]
        rotated = [mm(r, x).astype(BF16) for r, x in zip(rot, pair_density)]
        for p, r, x in zip(pairs, rot, rotated):
            part[p] = mm(x, r, 1, 1)

    z_last(1)
    last_copy.wait_recv()
    finish(1, 1, last_recv)
    z_last(0)
    x_copy(row).wait_recv()
    finish(0, 0, xrecv.at[row])

    def t_copy(d):
        t = (me + d) % n
        return remote(part_send.at[t], part_recv.at[me], t_send.at[d], t_recv.at[me], pair=t)

    def tile_part(t, j):
        total = jnp.where(tiles[0] == t * held + j, 1.0, 0.0).astype(F32) * part[0]
        for p in range(1, resident):
            total = total + jnp.where(tiles[p] == t * held + j, 1.0, 0.0).astype(F32) * part[p]
        return total

    def tile_send(d):
        t = (me + d) % n
        for j in range(held):
            part_send[t, j] = tile_part(t, j).astype(BF16)
        t_copy(d).start()

    loop(1, n, tile_send)
    for j in range(held):
        part_own[j] = tile_part(me, j)

    def tile_add(d):
        src = (me + d) % n
        here = part_recv.at[src]
        remote(here, here, t_send.at[0], t_recv.at[src], pair=src).wait_recv()
        for j in range(held):
            part_own[j] += part_recv[src, j].astype(F32)

    loop(1, n, tile_add)
    tot_send[...] = part_own[...].astype(BF16)

    def a_copy(d):
        return remote(tot_send, tot_recv.at[aux], a_send.at[d], a_recv.at[aux], aux=(aux + d) % n_aux)

    loop(1, n_aux, lambda d: a_copy(d).start())

    def tot_add(d):
        src = (aux + d) % n_aux
        here = tot_recv.at[src]
        remote(here, here, a_send.at[0], a_recv.at[src], aux=src).wait_recv()
        for j in range(held):
            part_own[j] += tot_recv[src, j].astype(F32)

    loop(1, n_aux, tot_add)
    for j in range(held):
        total[j] = part_own[j]

    def line_left(h):
        @pl.when((row + 1 < lines) & (h <= row))
        def _():
            up_copy(h).wait_send()
            up_late_copy(h).wait_send()

        @pl.when((row > 0) & (h >= row))
        def _():
            down_copy(h).wait_send()
            down_late_copy(h).wait_send()

        fwd_copy(h).wait_send()
        x_copy(h).wait_send()

        @pl.when(h > row)
        def _():
            for k in range(3):
                z_copy(k, h, True).wait_send()

        @pl.when(h < row)
        def _():
            for k in range(3):
                z_copy(k, h, False).wait_send()

    loop(0, lines, line_left)
    late_copy().wait_send()
    last_copy.wait_send()
    loop(1, n_aux, lambda d: block_copy(d).wait_send())
    loop(1, n, lambda d: t_copy(d).wait_send())
    loop(1, n_aux, lambda d: a_copy(d).wait_send())


def finishing(factor, fresh, total_in, coeffs_in, new_amps, density, coeffs, total, result, passing, sems):
    load = pltpu.make_async_copy(coeffs_in, coeffs, sems.at[0])
    load.start()
    sums = pltpu.make_async_copy(total_in, total, sems.at[2])
    sums.start()
    fetch = pltpu.make_async_copy(fresh, passing, sems.at[1])
    fetch.start()
    fetch.wait()
    keep = pltpu.make_async_copy(passing, new_amps, sems.at[3])
    keep.start()
    sums.wait()
    load.wait()
    held = coeffs.shape[0]
    stores = [pltpu.make_async_copy(result.at[j], density.at[j], sems.at[4 + j]) for j in range(held)]
    for j in range(held):
        high = total[j].astype(BF16)
        low = (total[j] - high.astype(F32)).astype(BF16)
        result[j] = (mm(high, coeffs[j]) + mm(low, coeffs[j])) * factor
        stores[j].start()
    for store in stores:
        store.wait()
    keep.wait()


def local(n, n_aux, amps, rotation, intersections, energies, domains, owners, slots, tiles, blocks, coeffs):
    resident, width = amps.shape[0], amps.shape[1]
    neighbours = owners.shape[1]
    entries = resident * neighbours
    lines = n // 2
    held = coeffs.shape[0]
    square = (width, width)
    dma = pltpu.SemaphoreType.DMA
    scratch = [
        (rotation.shape, BF16),
        ((entries,) + square, BF16),
        (energies.shape, F32),
        ((n * resident,) + square, BF16),
        ((n_aux * blocks.shape[0],) + blocks.shape[1:], BF16),
        ((entries,) + square, BF16),
        ((lines, resident // 2) + square, BF16),
        ((lines, resident // 2) + square, BF16),
        ((3, lines, resident // 2) + square, BF16),
        ((3, lines + 1, resident // 2) + square, BF16),
        ((resident // 2,) + square, BF16),
        ((resident // 2,) + square, BF16),
        ((resident,) + square, F32),
        ((resident,) + square, F32),
        ((resident,) + square, F32),
        ((resident,) + square, F32),
        ((held,) + square, F32),
        ((n, held) + square, BF16),
        ((n, held) + square, BF16),
        ((held,) + square, BF16),
        ((n_aux, held) + square, BF16),
    ]
    sems = [9] + [lines] * 6 + [lines + 1, lines, n_aux, n_aux, lines, lines, (3, lines), (3, lines + 1), 2]
    sems += [n, n, n_aux, n_aux]
    hbm = pl.BlockSpec(memory_space=pltpu.HBM)
    vmem = pl.BlockSpec(memory_space=pltpu.VMEM)
    out_shape = (
        jax.ShapeDtypeStruct(amps.shape, BF16),
        jax.ShapeDtypeStruct((held,) + square, F32),
    )
    fresh, total = pl.pallas_call(
        functools.partial(kernel, n, lines, n_aux, neighbours),
        out_shape=out_shape,
        in_specs=[hbm] * 9,
        out_specs=(vmem, vmem),
        scratch_shapes=[pltpu.SMEM(x.shape, jnp.int32) for x in (owners.T, slots.T, domains.T, tiles)]
        + [pltpu.VMEM(*s) for s in scratch]
        + [dma(k if isinstance(k, tuple) else (k,)) for k in sems],
        compiler_params=pltpu.CompilerParams(
            collective_id=0, has_side_effects=True, vmem_limit_bytes=60 << 20
        ),
    )(
        owners.T,
        slots.T,
        domains.T,
        tiles,
        amps,
        rotation,
        intersections.reshape((entries,) + square),
        energies,
        blocks,
    )
    return pl.pallas_call(
        functools.partial(finishing, 1.0 / (resident * n_aux)),
        out_shape=(
            jax.ShapeDtypeStruct(amps.shape, BF16),
            jax.ShapeDtypeStruct((held, width, coeffs.shape[2]), F32),
        ),
        in_specs=[hbm] * 3,
        out_specs=(hbm, hbm),
        scratch_shapes=[
            pltpu.VMEM(coeffs.shape, BF16),
            pltpu.VMEM((held,) + square, F32),
            pltpu.VMEM((held, width, coeffs.shape[2]), F32),
            pltpu.VMEM(amps.shape, BF16),
            dma((4 + held,)),
        ],
        compiler_params=pltpu.CompilerParams(vmem_limit_bytes=60 << 20),
    )(fresh, total, coeffs)


def solution(mesh):
    return jax.shard_map(
        functools.partial(local, mesh.shape["pair"], mesh.shape["aux"]),
        mesh=mesh,
        in_specs=(
            P(("pair", "aux"), None, None),
            P(("pair", "aux"), None, None),
            P(("pair", "aux"), None, None, None),
            P(("pair", "aux"), None),
            P(("pair", "aux"), None),
            P(("pair", "aux"), None),
            P(("pair", "aux"), None),
            P(("pair", "aux")),
            P("aux", None, None),
            P("pair", None, "aux"),
        ),
        out_specs=(P(("pair", "aux"), None, None), P("pair", None, "aux")),
        check_vma=False,
    )
```
